256 devices in a mesh: seq: 32 (over z_hi, x, core), tp: 8 (over y, z_lo).
Axes of the slice: x: 4, y: 4, z: 8 (z_hi: 4, z_lo: 2; z = z_hi * 2 + z_lo), core: 2. Of those that a mesh axis runs over, the one named last changes fastest.
Arguments:
- frame_grid: bfloat16 [64, 256, 8, 6, 128], P('seq', None, 'tp'), may hold values from -8 to 8
- keep_rows: int32 [64, 256], P('seq'), may hold values from 0 to 255, as said below
- kept_count: int32 [64], replicated, may hold values from 36 to 220, as said below
- frame_slot: int32 [64], replicated, may hold values from 0 to 63, as said below
- out_weight: bfloat16 [4096, 8192], P('tp'), may hold values from -0.125 to 0.125
- residual: bfloat16 [8192, 8192], P('seq', 'tp'), may hold values from -48 to 48
- norm_gain: bfloat16 [8192], P('tp'), may hold values from 0.5 to 1.5
Outputs:
- hidden: bfloat16 [8192, 8192], P('seq', 'tp')
- normed: bfloat16 [8192, 8192], P('seq', 'tp')
The draws below stay inside these ranges and needn't reach their ends.
Inputs may be any that keep to these rules, and one draw needn't show every extreme that they name: `kept_count`: frames follow one another in the sequence in the order of f; the counts sum to 8192. `frame_slot`: each slot holds exactly one frame. `keep_rows`: in the slot of frame f the first kept_count[f] entries are distinct grid rows in ascending order; the other entries are the remaining rows.
All inputs are finite; a program needn't handle non-finite values.
Results may differ from the reference program's by a relative error of at most 0.009.
Values may be sent and summed in bfloat16 or wider, within the bound.
A program may use at most 192 MiB of HBM per device.

```python
import math
import jax
import jax.numpy as jnp
from jax import lax

D = 8192
QH = 32
KVH = 8
HD = 128
GRID = 256
FR_DEV = 2
QPK = 4
KEEP_LEAST = 36
TOK_DEV = 256
FRAMES = 64
TOKENS = 8192
N_SEQ = 32
N_TP = 8


def frame_layout(key):
    split_keys = jax.random.split(key, 5)
    spread = GRID // 2 - KEEP_LEAST
    lift_values = jax.random.randint(split_keys[0], (FRAMES,), 0, spread + 1)
    leading = jax.random.randint(split_keys[1], (), 0, FRAMES)
    partner = (leading + 2 + jax.random.randint(split_keys[2], (), 0, FRAMES - 3)) % FRAMES
    lowered = jnp.stack([(leading + 1) % FRAMES, (partner + 1) % FRAMES])
    raised = jnp.stack([leading, (leading + 2) % FRAMES, partner])
    lift_values = lift_values.at[lowered].set(0).at[raised].set(spread)
    counts = GRID // 2 + lift_values - jnp.roll(lift_values, -1)
    ranking = jax.random.permutation(split_keys[3], FRAMES)
    ranking = ranking.at[leading].set(-2).at[partner].set(-1)
    frame_order = jnp.argsort(ranking, stable=True)
    offset = FR_DEV * jax.random.randint(split_keys[4], (), 0, FRAMES // FR_DEV)
    slot_ids = jnp.zeros((FRAMES,), jnp.int32).at[frame_order].set(((jnp.arange(FRAMES) + offset) % FRAMES).astype(jnp.int32))
    return (counts.astype(jnp.int32), slot_ids)


def draw_kept_count(key, part):
    return frame_layout(key)[0]


def draw_frame_slot(key, part):
    return frame_layout(key)[1]


def draw_keep_rows(key, part):
    counts, slot_ids = frame_layout(key)
    key = jax.random.fold_in(key, 7)
    holder = jnp.zeros((FRAMES,), jnp.int32).at[slot_ids].set(jnp.arange(FRAMES, dtype=jnp.int32))
    slot_counts = counts[holder]
    ranking = jax.vmap(lambda subkey: jax.random.permutation(subkey, GRID))(jax.random.split(key, FRAMES))
    grid_ids = jnp.arange(GRID, dtype=jnp.int32)[None, :]
    scores = jnp.where(ranking < slot_counts[:, None], grid_ids, GRID + grid_ids)
    return jnp.argsort(scores, axis=1, stable=True).astype(jnp.int32)


def draw_frame_grid(key, part):
    key = jax.random.fold_in(key, 11)
    base_key = jax.random.fold_in(key, 0)
    grid_shape = (FRAMES, GRID, KVH, QPK + 2, HD)
    scales = jnp.where(jnp.arange(QPK + 2) < QPK + 1, 1.75, 1.0)[None, None, None, :, None]
    values = jnp.clip(jax.random.normal(base_key, grid_shape, jnp.float32) * scales, -8.0, 8.0)
    return values.astype(jnp.bfloat16)


def draw_residual(key, part):
    key = jax.random.fold_in(key, 13)
    base_key, row_key, column_key = jax.random.split(key, 3)
    row_scale = 10.0 ** jax.random.uniform(row_key, (TOKENS, 1), jnp.float32)
    column_scale = 10.0 ** jax.random.uniform(column_key, (1, D), jnp.float32) * 3.0 ** (jnp.arange(D, dtype=jnp.float32)[None, :] / D)
    values = jnp.clip(jax.random.normal(base_key, (TOKENS, D), jnp.float32), -4.0, 4.0)
    return (0.04 * values * row_scale * column_scale).astype(jnp.bfloat16)


def strengthened(entries, key, source, target, blocks, factor):
    def block_of(axis_at):
        return (jnp.arange(entries.shape[axis_at]) // (entries.shape[axis_at] // blocks)).reshape((-1,) + (1,) * (entries.ndim - 1 - axis_at))

    near = jax.random.permutation(key, blocks)[block_of(target)]
    other_side = (block_of(target) + blocks // 2) % blocks
    return jnp.where((block_of(source) == near) | (block_of(source) == other_side), factor * entries, entries)


def block_scale(stream_key, dims, shards, low, largest):
    gain = 1.0
    for dim, shards_of in shards:
        draws = jax.random.uniform(jax.random.fold_in(jax.random.fold_in(stream_key, 6), dim), (shards_of,), jnp.float32, low / len(shards), largest / len(shards))
        gain = gain * jnp.repeat(jnp.exp(draws), dims[dim] // shards_of).reshape((-1,) + (1,) * (len(dims) - 1 - dim))
    return gain


def bell_draw_with(rng, dims, deviation, most, cuts, heavy, kind=jnp.bfloat16):
    drawn = deviation * jax.random.normal(rng, dims, jnp.float32)
    if cuts:
        drawn = drawn * block_scale(rng, dims, cuts, -0.22, 0.18)
    return jnp.clip(strengthened(drawn, jax.random.fold_in(rng, 3), *heavy), -most, most).astype(kind)


def setup_inputs(seed: int = 0) -> dict:
    streams_of = jax.random.split(jax.random.key(seed), 8)
    frame_grid = draw_frame_grid(jax.random.fold_in(streams_of[7], 71), 0)
    keep_rows = draw_keep_rows(jax.random.fold_in(streams_of[7], 71), 0)
    kept_count = draw_kept_count(jax.random.fold_in(streams_of[7], 71), 0)
    frame_slot = draw_frame_slot(jax.random.fold_in(streams_of[7], 71), 0)
    out_weight = bell_draw_with(streams_of[4], (QH * HD, D), (QH * HD) ** -0.5, 0.125, ((0, 8),), (0, 1, 8, 2.0))
    residual = draw_residual(jax.random.fold_in(streams_of[7], 71), 0)
    norm_gain = jnp.clip(1.0 + 0.1 * jax.random.normal(streams_of[6], (D,), jnp.float32), 0.5, 1.5).astype(jnp.bfloat16)
    return dict(frame_grid=frame_grid, keep_rows=keep_rows, kept_count=kept_count, frame_slot=frame_slot, out_weight=out_weight, residual=residual, norm_gain=norm_gain)


def reference(frame_grid, keep_rows, kept_count, frame_slot, out_weight, residual, norm_gain):
    starts = (jnp.cumsum(kept_count) - kept_count).astype(jnp.int32)
    frame_ends = (starts + kept_count).astype(jnp.int32)
    positions = jnp.arange(TOKENS, dtype=jnp.int32)
    frame_ids = lax.optimization_barrier(jnp.sum((positions[:, None] >= frame_ends[None, :]).astype(jnp.int32), axis=1)).astype(jnp.int32)
    within = (positions - starts[frame_ids]).astype(jnp.int32)
    slot_pick = frame_slot[frame_ids].astype(jnp.int32)
    grid_pick = keep_rows[slot_pick, within].astype(jnp.int32)
    flat_grid = frame_grid.reshape(FRAMES * GRID, KVH, QPK + 2, HD)
    tokens = flat_grid[(slot_pick * GRID + grid_pick).astype(jnp.int32)]
    queries = tokens[:, :, :QPK]
    key_rows = jnp.moveaxis(tokens[:, :, QPK], 1, 0)
    value_rows = jnp.moveaxis(tokens[:, :, QPK + 1], 1, 0)
    score_scale = 1.0 / math.sqrt(HD)
    block_rows = min(512, TOKENS)

    def one_block(number):
        query_rows = lax.dynamic_slice_in_dim(queries, number * block_rows, block_rows, 0)
        query_frames = lax.dynamic_slice_in_dim(frame_ids, number * block_rows, block_rows, 0)
        visible = frame_ids[None, :] <= query_frames[:, None]

        def one_group(operands):
            group_queries, group_keys, group_values = operands
            scores = jnp.einsum('qah,kh->aqk', group_queries.astype(jnp.float32), group_keys.astype(jnp.float32)) * score_scale
            scores = jnp.where(visible[None], scores, -jnp.inf)
            weights = jnp.exp(scores - lax.optimization_barrier(jnp.max(scores, axis=-1, keepdims=True)))
            denominator = lax.optimization_barrier(jnp.sum(weights, axis=-1, keepdims=True))
            rounded = lax.optimization_barrier(weights.astype(jnp.bfloat16)).astype(jnp.float32)
            summed = jnp.einsum('aqk,kh->aqh', rounded, group_values.astype(jnp.float32))
            return summed / denominator
        grouped = lax.map(one_group, (jnp.moveaxis(query_rows, 1, 0), key_rows, value_rows))
        return grouped.transpose(2, 0, 1, 3).reshape(block_rows, QH * HD).astype(jnp.bfloat16)
    attended = lax.map(one_block, jnp.arange(TOKENS // block_rows, dtype=jnp.int32)).reshape(TOKENS, QH * HD)
    heads_each = QH * HD // N_TP
    attended_parts = attended.reshape(TOKENS, N_TP, heads_each).transpose(1, 0, 2)
    weight_parts = out_weight.reshape(N_TP, heads_each, D)

    def add_part(carried, pieces):
        partial_value = jnp.dot(pieces[0], pieces[1], preferred_element_type=jnp.float32)
        return (carried + lax.optimization_barrier(partial_value.astype(jnp.bfloat16)).astype(jnp.float32), None)
    attention = lax.scan(add_part, jnp.zeros((TOKENS, D), jnp.float32), (attended_parts, weight_parts))[0]
    residual_ordered = residual.reshape(N_SEQ, TOK_DEV, D).transpose(1, 0, 2).reshape(TOKENS, D)
    stream = residual_ordered.astype(jnp.float32) + attention
    mean_square = lax.optimization_barrier(jnp.mean(stream * stream, axis=1, keepdims=True))
    normed = (stream * lax.rsqrt(mean_square + 1e-06) * norm_gain.astype(jnp.float32)[None, :]).astype(jnp.bfloat16)
    hidden = stream.astype(jnp.bfloat16)
    hidden = hidden.reshape(TOK_DEV, N_SEQ, D).transpose(1, 0, 2).reshape(TOKENS, D)
    normed = normed.reshape(TOK_DEV, N_SEQ, D).transpose(1, 0, 2).reshape(TOKENS, D)
    return (hidden, normed)
```

```python
import functools
import math

import jax
import jax.numpy as jnp
import numpy as np
from jax import lax
from jax.experimental import pallas as pl
from jax.experimental.pallas import tpu as pltpu
from jax.sharding import PartitionSpec as P

D = 8192
HD = 128
HEADS = 4
FRAMES = 64
GRID = 256
TOK = 256
N_SEQ = 32
N_TP = 8
WIDTH = D // N_TP
PAIR = 16
CHUNKS = 4
ROWS = TOK // CHUNKS
KEY_AT = (0, 80, 144, 208, 256)
KEY_ROWS = tuple(KEY_AT[i + 1] - KEY_AT[i] for i in range(CHUNKS))
KEY_BLOCK = 1024
NEGATIVE = -1e30
EPSILON = 1e-06
SCALE = 1.0 / math.sqrt(HD)
MESH = pl.DeviceIdType.MESH
F32 = jnp.float32
BF16 = jnp.bfloat16


def key_positions():
    out = []
    for chunk in range(CHUNKS):
        x, c, z, l = np.meshgrid(
            np.arange(4), np.arange(2), np.arange(4), np.arange(KEY_AT[chunk], KEY_AT[chunk + 1]), indexing="ij"
        )
        out.append((l * N_SEQ + (z * 4 + x) * 2 + c).reshape(-1))
    return np.concatenate(out).astype(np.int32)[None, :]


def iota(shape, dim):
    return lax.broadcasted_iota(jnp.int32, shape, dim)


def one_hot(mask):
    return jnp.where(mask, 1.0, 0.0).astype(BF16)


def dot(a, b, contract):
    return lax.dot_general(a, b, ((contract[:1], contract[1:]), ((), ())), preferred_element_type=F32)


def kernel(
    x_ref, keep_ref, count_ref, slot_ref, kpos_ref, w_hbm, res_ref, gain_ref,
    hid_ref, nrm_ref,
    send_kv, send_q, recv_kv, recv_q, kv0, kv1, kv2, kv3, q_ref, w_ref,
    m_ref, den_ref, acc_ref, att_ref, part_ref, half_p, half_m, block_p, block_m,
    z_send, z_recv, stream_ref, ssq_ref, ssq_send, ssq_recv,
    a2a_sem, g_send, g_recv, r_send, r_recv, s_sem, w_sem,
):
    kvs = (kv0, kv1, kv2, kv3)
    me = lax.axis_index("seq")
    tp = lax.axis_index("tp")
    zz, xx, cc = me >> 3, (me >> 1) & 3, me & 1
    yy, zl = tp >> 1, tp & 1

    def seq_id(z, x, c):
        return {"seq": (((z & 3) * 4 + (x & 3)) * 2 + c)}

    def tp_id(y, z):
        return {"tp": (y & 3) * 2 + z}

    w_copy = pltpu.make_async_copy(w_hbm, w_ref, w_sem)
    w_copy.start()

    barrier = pltpu.get_barrier_semaphore()

    @pl.loop(1, N_SEQ)
    def _(o):
        pl.semaphore_signal(barrier, inc=1, device_id={"seq": (me + o) & 31}, device_id_type=MESH)

    @pl.loop(1, N_TP)
    def _(o):
        pl.semaphore_signal(barrier, inc=1, device_id={"tp": (tp + o) & 7}, device_id_type=MESH)

    f_col, f_row = iota((FRAMES, FRAMES), 0), iota((FRAMES, FRAMES), 1)
    counts, slots = count_ref[...], slot_ref[...]
    starts_col = jnp.sum(jnp.where(f_row < f_col, counts, 0), axis=1, keepdims=True)
    count_col = jnp.sum(jnp.where(f_row == f_col, counts, 0), axis=1, keepdims=True)
    slot_col = jnp.sum(jnp.where(f_row == f_col, slots, 0), axis=1, keepdims=True)
    ends_row = jnp.sum(jnp.where(f_col <= f_row, count_col, 0), axis=0, keepdims=True)

    r_id = iota((N_SEQ * PAIR, 1), 0)
    second = ((r_id >> 3) & 1) == 1

    def own(fl, values):
        return jnp.sum(jnp.where(slot_col == 2 * me + fl, values, 0), axis=0, keepdims=True)

    first_r = jnp.where(second, own(1, starts_col), own(0, starts_col))
    count_r = jnp.where(second, own(1, count_col), own(0, count_col))
    offset_r = (((r_id >> 4) - first_r) & 31) + 32 * (r_id & 7)
    offset_r = jnp.where(offset_r < count_r, offset_r, -1)
    picked = []
    for fl in range(2):
        wanted = jnp.where(second if fl else jnp.logical_not(second), offset_r, -1)
        chosen = one_hot(iota((N_SEQ * PAIR, GRID), 1) == wanted)
        kept = one_hot(iota((GRID, GRID), 0) == keep_ref[fl : fl + 1, :])
        picked.append(dot(chosen, kept, (1, 1)).astype(BF16))
    pick = jnp.concatenate(picked, axis=1)
    send_kv[...] = dot(pick, x_ref[:, HEADS * HD :], (1, 0)).astype(BF16).reshape(N_SEQ, PAIR, 2 * HD)

    pl.semaphore_wait(barrier, N_SEQ - 1 + N_TP - 1)

    def exchange(src, dst, at):
        @pl.loop(1, N_SEQ)
        def _(o):
            other = (me + o) & 31
            pltpu.make_async_remote_copy(
                src_ref=src.at[other],
                dst_ref=dst.at[me],
                send_sem=a2a_sem.at[at],
                recv_sem=a2a_sem.at[at + 1],
                device_id={"seq": other},
                device_id_type=MESH,
            ).start()

    def exchange_all(src, dst, at):
        return pltpu.make_async_remote_copy(
            src_ref=src.at[pl.ds(0, N_SEQ - 1)],
            dst_ref=dst.at[pl.ds(0, N_SEQ - 1)],
            send_sem=a2a_sem.at[at],
            recv_sem=a2a_sem.at[at + 1],
            device_id={"seq": (me + 1) & 31},
            device_id_type=MESH,
        )

    exchange(send_kv, recv_kv, 0)
    recv_kv[pl.ds(me, 1)] = send_kv[pl.ds(me, 1)]
    send_q[...] = dot(pick, x_ref[:, : HEADS * HD], (1, 0)).astype(BF16).reshape(N_SEQ, PAIR, HEADS * HD)

    lane = iota((1, N_SEQ * PAIR), 1)
    at_slot = slot_col == (iota((FRAMES, N_SEQ * PAIR), 1) >> 3)
    first_l = jnp.sum(jnp.where(at_slot, starts_col, 0), axis=0, keepdims=True)
    count_l = jnp.sum(jnp.where(at_slot, count_col, 0), axis=0, keepdims=True)
    offset_l = ((me - first_l) & 31) + 32 * (lane & 7)
    row_l = jnp.where(offset_l < count_l, (first_l + offset_l) >> 5, -1)
    place = one_hot(iota((TOK, N_SEQ * PAIR), 0) == row_l)
    q_pos = iota((TOK, 1), 0) * N_SEQ + me
    ends = jnp.min(jnp.where(ends_row > q_pos, ends_row, 2 * D), axis=1, keepdims=True)

    kv_all = exchange_all(send_kv, recv_kv, 0)
    kv_all.wait_recv()
    mine = dot(place, recv_kv[...].reshape(N_SEQ * PAIR, 2 * HD), (1, 0)).astype(BF16)
    for c in range(CHUNKS):
        kvs[c][xx, cc, zz] = mine[KEY_AT[c] : KEY_AT[c + 1], :]

    def seq_copy(c, at, src, dst, device):
        return pltpu.make_async_remote_copy(
            src_ref=src, dst_ref=dst, send_sem=g_send.at[c, at], recv_sem=g_recv.at[c, at],
            device_id=device, device_id_type=MESH,
        )

    def z_one(c):
        ref = kvs[c].at[xx, cc, zz]
        return [
            seq_copy(c, 0, ref, ref, seq_id(zz + 1, xx, cc)),
            seq_copy(c, 1, ref, ref, seq_id(zz - 1, xx, cc)),
        ]

    def z_two(c):
        cut = KEY_ROWS[c] // 32 * 16
        up = kvs[c].at[xx, cc, (zz - 1) & 3, pl.ds(0, cut)]
        down = kvs[c].at[xx, cc, (zz + 1) & 3, pl.ds(cut, KEY_ROWS[c] - cut)]
        return [
            seq_copy(c, 2, up, up, seq_id(zz + 1, xx, cc)),
            seq_copy(c, 3, down, down, seq_id(zz - 1, xx, cc)),
        ]

    def x_one(c):
        ref = kvs[c].at[xx, cc]
        return [
            seq_copy(c, 4, ref, ref, seq_id(zz, xx + 1, cc)),
            seq_copy(c, 5, ref, ref, seq_id(zz, xx - 1, cc)),
        ]

    def x_two(c):
        up = kvs[c].at[(xx - 1) & 3, cc, pl.ds(0, 2)]
        down = kvs[c].at[(xx + 1) & 3, cc, pl.ds(2, 2)]
        return [
            seq_copy(c, 6, up, up, seq_id(zz, xx + 1, cc)),
            seq_copy(c, 7, down, down, seq_id(zz, xx - 1, cc)),
        ]

    def sibling(c, step):
        ref = kvs[c].at[(xx + step) & 3, cc]
        return [seq_copy(c, 8 + step, ref, ref, seq_id(zz, xx, 1 - cc))]

    def start(copies):
        for copy in copies:
            copy.start()

    def wait_recv(copies):
        for copy in copies:
            copy.wait_recv()

    def wait_send(copies):
        for copy in copies:
            copy.wait_send()

    def gather_stage(stage, c):
        if stage == 1:
            wait_recv(z_one(c))
            start(z_two(c))
        elif stage == 2:
            wait_recv(z_two(c))
            start(x_one(c))
            start(sibling(c, 0))
        elif stage == 3:
            wait_recv(x_one(c))
            start(x_two(c))
            start(sibling(c, 1))
            start(sibling(c, 3))
        elif stage == 4:
            wait_recv(x_two(c))
            start(sibling(c, 2))
        elif stage == 5:
            for step in range(4):
                wait_recv(sibling(c, step))

    for c in range(CHUNKS):
        start(z_one(c))
    exchange(send_q, recv_q, 2)
    recv_q[pl.ds(me, 1)] = send_q[pl.ds(me, 1)]

    def load_queries():
        exchange_all(send_q, recv_q, 2).wait_recv()
        queries = dot(place, recv_q[...].reshape(N_SEQ * PAIR, HEADS * HD), (1, 0)).astype(BF16)
        for a in range(HEADS):
            q_ref[a] = queries[:, a * HD : (a + 1) * HD]

    def attention(j):
        q = q_ref[:, j * ROWS : (j + 1) * ROWS, :].reshape(HEADS * ROWS, HD)
        end = jnp.concatenate([ends[j * ROWS : (j + 1) * ROWS]] * HEADS, axis=0)
        m_ref[...] = jnp.full_like(m_ref, NEGATIVE)
        den_ref[...] = jnp.zeros_like(den_ref)
        acc_ref[...] = jnp.zeros_like(acc_ref)
        for c in range(j + 1):
            total = KEY_ROWS[c] * N_SEQ
            block = total // (total // KEY_BLOCK)
            flat = kvs[c].reshape(total, 2 * HD)

            @pl.loop(0, total // block)
            def _(i, c=c, block=block, flat=flat):
                at = pl.multiple_of(i * block, 128)
                keys = flat[pl.ds(at, block), :HD]
                values = flat[pl.ds(at, block), HD:]
                s = dot(q, keys, (1, 1))
                if c >= j - 1:
                    pos = kpos_ref[:, pl.ds(pl.multiple_of(KEY_AT[c] * N_SEQ + at, 128), block)]
                    s = jnp.where(pos < end, s, NEGATIVE)
                old = m_ref[:, :1]
                new = jnp.maximum(old, jnp.max(s, axis=1, keepdims=True))
                p = jnp.exp((s - new) * SCALE)
                keep = jnp.exp((old - new) * SCALE)
                m_ref[...] = jnp.broadcast_to(new, m_ref.shape)
                den_ref[...] = den_ref[...] * keep + jnp.sum(p, axis=1, keepdims=True)
                acc_ref[...] = acc_ref[...] * keep + dot(p.astype(BF16), values, (1, 0))

        out = (acc_ref[...] / den_ref[...]).astype(BF16)
        att_ref[...] = jnp.concatenate([out[a * ROWS : (a + 1) * ROWS] for a in range(HEADS)], axis=1)

    def tp_copy(j, at, src, dst, device):
        return pltpu.make_async_remote_copy(
            src_ref=src, dst_ref=dst, send_sem=r_send.at[j, at], recv_sem=r_recv.at[j, at],
            device_id=device, device_id_type=MESH,
        )

    y_up, y_down, y_far = (yy + 1) & 3, (yy - 1) & 3, (yy + 2) & 3

    def far_halves(j):
        return [
            tp_copy(j, 0, part_ref.at[j, 2 * y_far], half_p.at[j], tp_id(yy + 1, zl)),
            tp_copy(j, 1, part_ref.at[j, 2 * y_far + 1], half_m.at[j], tp_id(yy - 1, zl)),
        ]

    def near_blocks(j):
        return [
            tp_copy(j, 2, part_ref.at[j, pl.ds(2 * y_up, 2)], block_p.at[j], tp_id(yy + 1, zl)),
            tp_copy(j, 3, part_ref.at[j, pl.ds(2 * y_down, 2)], block_m.at[j], tp_id(yy - 1, zl)),
        ]

    def z_pair(j):
        return [tp_copy(j, 4, z_send.at[j], z_recv.at[j], tp_id(yy, 1 - zl))]

    def project(j):
        def columns(y):
            @pl.loop(0, 2)
            def _(h):
                t = 2 * y + h
                w = w_ref[:, pl.ds(pl.multiple_of(t * WIDTH, WIDTH), WIDTH)]
                part_ref[j, t] = dot(att_ref[...], w, (1, 0)).astype(BF16)

        columns(y_far)
        start(far_halves(j))
        columns(y_up)
        columns(y_down)
        columns(yy)

    def reduce_near(j):
        wait_recv(far_halves(j))
        part_ref[j, 2 * y_up] = (part_ref[j, 2 * y_up].astype(F32) + half_p[j].astype(F32)).astype(BF16)
        part_ref[j, 2 * y_down + 1] = (part_ref[j, 2 * y_down + 1].astype(F32) + half_m[j].astype(F32)).astype(BF16)
        start(near_blocks(j))

    def reduce_own(j):
        wait_recv(near_blocks(j))

        def total(h):
            return part_ref[j, 2 * yy + h].astype(F32) + block_p[j, h].astype(F32) + block_m[j, h].astype(F32)

        z_send[j] = total(1 - zl).astype(BF16)
        start(z_pair(j))
        rows = pl.ds(j * ROWS, ROWS)
        stream_ref[rows, :] = total(zl) + res_ref[rows, :].astype(F32)

    def finish_rows(j):
        wait_recv(z_pair(j))
        rows = pl.ds(j * ROWS, ROWS)
        stream = stream_ref[rows, :] + z_recv[j].astype(F32)
        stream_ref[rows, :] = stream
        hid_ref[rows, :] = stream.astype(BF16)
        ssq_ref[rows, :] = jnp.broadcast_to(jnp.sum(stream * stream, axis=1, keepdims=True), (ROWS, HD))

    gather_stage(1, 0)
    gather_stage(2, 0)
    gather_stage(1, 1)
    gather_stage(3, 0)
    gather_stage(2, 1)
    gather_stage(1, 2)
    gather_stage(4, 0)
    gather_stage(3, 1)
    gather_stage(2, 2)
    gather_stage(1, 3)
    load_queries()
    gather_stage(5, 0)
    gather_stage(4, 1)
    gather_stage(3, 2)
    gather_stage(2, 3)
    attention(0)
    w_copy.wait()
    project(0)
    gather_stage(5, 1)
    gather_stage(4, 2)
    gather_stage(3, 3)
    attention(1)
    reduce_near(0)
    project(1)
    gather_stage(5, 2)
    gather_stage(4, 3)
    attention(2)
    reduce_near(1)
    reduce_own(0)
    project(2)
    gather_stage(5, 3)
    attention(3)
    reduce_near(2)
    reduce_own(1)
    project(3)
    finish_rows(0)
    reduce_near(3)
    reduce_own(2)
    finish_rows(1)
    reduce_own(3)
    finish_rows(2)
    finish_rows(3)

    diag = iota((TOK, TOK), 0) == iota((TOK, TOK), 1)
    ssq_row = jnp.sum(jnp.where(diag, ssq_ref[:, :1], 0.0), axis=0, keepdims=True)
    ssq_send[...] = jnp.broadcast_to(ssq_row, (8, TOK))
    ssq_recv[pl.ds(tp, 1)] = ssq_send[...][None]

    @pl.loop(1, N_TP)
    def _(o):
        pltpu.make_async_remote_copy(
            src_ref=ssq_send, dst_ref=ssq_recv.at[tp], send_sem=s_sem.at[0], recv_sem=s_sem.at[1],
            device_id={"tp": (tp + o) & 7}, device_id_type=MESH,
        ).start()

    ssq_all = pltpu.make_async_remote_copy(
        src_ref=ssq_recv.at[pl.ds(0, N_TP - 1)], dst_ref=ssq_recv.at[pl.ds(0, N_TP - 1)],
        send_sem=s_sem.at[0], recv_sem=s_sem.at[1],
        device_id={"tp": (tp + 1) & 7}, device_id_type=MESH,
    )
    ssq_all.wait_recv()
    sums = jnp.sum(ssq_recv[...], axis=0)[:1, :]
    inverse_row = lax.rsqrt(sums / D + EPSILON)
    inverse = jnp.sum(jnp.where(diag, inverse_row, 0.0), axis=1, keepdims=True)
    nrm_ref[...] = (stream_ref[...] * inverse * gain_ref[...].astype(F32)).astype(BF16)

    ssq_all.wait_send()
    kv_all.wait_send()
    exchange_all(send_q, recv_q, 2).wait_send()
    for c in range(CHUNKS):
        wait_send(z_one(c) + z_two(c) + x_one(c) + x_two(c))
        for step in range(4):
            wait_send(sibling(c, step))
        wait_send(far_halves(c) + near_blocks(c) + z_pair(c))


def body(frame_grid, keep_rows, kept_count, frame_slot, out_weight, residual, norm_gain):
    vmem = pl.BlockSpec(memory_space=pltpu.VMEM)
    dma = pltpu.SemaphoreType.DMA
    return pl.pallas_call(
        kernel,
        out_shape=[jax.ShapeDtypeStruct((TOK, WIDTH), BF16)] * 2,
        in_specs=[vmem] * 5 + [pl.BlockSpec(memory_space=pl.ANY)] + [vmem] * 2,
        out_specs=[vmem] * 2,
        scratch_shapes=[
            pltpu.VMEM((N_SEQ, PAIR, 2 * HD), BF16),
            pltpu.VMEM((N_SEQ, PAIR, HEADS * HD), BF16),
            pltpu.VMEM((N_SEQ, PAIR, 2 * HD), BF16),
            pltpu.VMEM((N_SEQ, PAIR, HEADS * HD), BF16),
        ]
        + [pltpu.VMEM((4, 2, 4, rows, 2 * HD), BF16) for rows in KEY_ROWS]
        + [
            pltpu.VMEM((HEADS, TOK, HD), BF16),
            pltpu.VMEM((HEADS * HD, D), BF16),
            pltpu.VMEM((HEADS * ROWS, HD), F32),
            pltpu.VMEM((HEADS * ROWS, HD), F32),
            pltpu.VMEM((HEADS * ROWS, HD), F32),
            pltpu.VMEM((ROWS, HEADS * HD), BF16),
            pltpu.VMEM((CHUNKS, N_TP, ROWS, WIDTH), BF16),
            pltpu.VMEM((CHUNKS, ROWS, WIDTH), BF16),
            pltpu.VMEM((CHUNKS, ROWS, WIDTH), BF16),
            pltpu.VMEM((CHUNKS, 2, ROWS, WIDTH), BF16),
            pltpu.VMEM((CHUNKS, 2, ROWS, WIDTH), BF16),
            pltpu.VMEM((CHUNKS, ROWS, WIDTH), BF16),
            pltpu.VMEM((CHUNKS, ROWS, WIDTH), BF16),
            pltpu.VMEM((TOK, WIDTH), F32),
            pltpu.VMEM((TOK, HD), F32),
            pltpu.VMEM((8, TOK), F32),
            pltpu.VMEM((N_TP, 8, TOK), F32),
            dma((4,)),
            dma((CHUNKS, 12)),
            dma((CHUNKS, 12)),
            dma((CHUNKS, 5)),
            dma((CHUNKS, 5)),
            dma((2,)),
            dma,
        ],
        compiler_params=pltpu.CompilerParams(
            collective_id=0, has_side_effects=True, vmem_limit_bytes=56 * 1024 * 1024
        ),
        cost_estimate=pl.CostEstimate(flops=5 * 10**9, bytes_accessed=12 * 10**6, transcendentals=5 * 10**6),
    )(
        frame_grid.reshape(2 * GRID, (HEADS + 2) * HD),
        keep_rows,
        kept_count.reshape(1, FRAMES),
        frame_slot.reshape(1, FRAMES),
        jnp.asarray(key_positions()),
        out_weight,
        residual,
        norm_gain.reshape(1, WIDTH),
    )


def solution(mesh):
    in_specs = (
        P("seq", None, "tp", None, None),
        P("seq", None),
        P(),
        P(),
        P("tp", None),
        P("seq", "tp"),
        P("tp"),
    )
    out_specs = (P("seq", "tp"), P("seq", "tp"))
    return jax.shard_map(body, mesh=mesh, in_specs=in_specs, out_specs=out_specs, check_vma=False)
```

```python
import math

import jax
import jax.numpy as jnp
from jax import lax
from jax.experimental import pallas as pl
from jax.experimental.pallas import tpu as pltpu
from jax.sharding import PartitionSpec as P

D = 8192
HD = 128
HEADS = 4
FRAMES = 64
GRID = 256
TOK = 256
N_SEQ = 32
N_TP = 8
WIDTH = D // N_TP
PAIR = 16
QUERY_AT = (0, 64, 128, 192, 256)
KEY_AT = (0, 80, 144, 208, 256)
CHUNKS = 4
KEY_ROWS = tuple(KEY_AT[i + 1] - KEY_AT[i] for i in range(CHUNKS))
KEY_BLOCKS = (1, 1, 1, 1)
MOST = max(QUERY_AT[i + 1] - QUERY_AT[i] for i in range(CHUNKS))
UNIT = 32
UNITS = TOK // UNIT
PAIR_FIRST = (False, True, False, True, False, True, False, True)
UNITS_OF = ((0, 1), (2, 3), (4, 5), (6, 7))
X_DIRECT = False
NEGATIVE = -1e30
FAR = 1 << 20
EPSILON = 1e-06
SCALE = math.log2(math.e) / math.sqrt(HD)
MESH = pl.DeviceIdType.MESH
F32 = jnp.float32
BF16 = jnp.bfloat16


def iota(shape, dim):
    return lax.broadcasted_iota(jnp.int32, shape, dim)


def one_hot(mask):
    return jnp.where(mask, 1.0, 0.0).astype(BF16)


def dot(a, b, contract):
    return lax.dot_general(a, b, ((contract[:1], contract[1:]), ((), ())), preferred_element_type=F32)


def kernel(
    x_ref, keep_ref, count_ref, slot_ref, w_hbm, res_ref,
    stream_ref, inverse_ref,
    send_kv, send_q, recv_kv, recv_q, kv0, kv1, kv2, kv3, seen0, seen1, seen2, seen3, q_ref, bias_ref, w_ref,
    m_ref, acc_ref, att_ref, part_ref, pair_ref, half_send, half_p, half_m, near_send, block_p, block_m,
    z_send, z_recv, ssq_ref, ssq_send, ssq_recv,
    a2a_sem, g_send, g_recv, r_send, r_recv, s_sem, w_sem,
):
    kvs, seen = (kv0, kv1, kv2, kv3), (seen0, seen1, seen2, seen3)
    me = lax.axis_index("seq")
    tp = lax.axis_index("tp")
    zz, xx, cc = me >> 3, (me >> 1) & 3, me & 1
    yy, zl = tp >> 1, tp & 1
    y_up, y_down, y_far = (yy + 1) & 3, (yy - 1) & 3, (yy + 2) & 3

    def seq_id(z, x, c):
        return {"seq": (((z & 3) * 4 + (x & 3)) * 2 + c)}

    def tp_id(y, z):
        return {"tp": (y & 3) * 2 + z}

    to_send, to_recv = {}, {}

    def start(copies):
        for key, copy in copies:
            copy.start()
            to_send[key] = to_recv[key] = copy

    def wait_recv(copies):
        for key, copy in copies:
            copy.wait_recv()
            to_recv.pop(key)

    w_copy = pltpu.make_async_copy(w_hbm, w_ref, w_sem)
    w_copy.start()

    barrier = pltpu.get_barrier_semaphore()

    @pl.loop(1, N_SEQ)
    def _(o):
        pl.semaphore_signal(barrier, inc=1, device_id={"seq": (me + o) & 31}, device_id_type=MESH)

    @pl.loop(1, N_TP)
    def _(o):
        pl.semaphore_signal(barrier, inc=1, device_id={"tp": (tp + o) & 7}, device_id_type=MESH)

    f_col, f_row = iota((FRAMES, FRAMES), 0), iota((FRAMES, FRAMES), 1)
    counts, slots = count_ref[...], slot_ref[...]
    starts_col = jnp.sum(jnp.where(f_row < f_col, counts, 0), axis=1, keepdims=True)
    count_col = jnp.sum(jnp.where(f_row == f_col, counts, 0), axis=1, keepdims=True)
    slot_col = jnp.sum(jnp.where(f_row == f_col, slots, 0), axis=1, keepdims=True)

    r_id = iota((N_SEQ * PAIR, 1), 0)
    second = ((r_id >> 3) & 1) == 1

    def own(fl, values):
        return jnp.sum(jnp.where(slot_col == 2 * me + fl, values, 0), axis=0, keepdims=True)

    first_r = jnp.where(second, own(1, starts_col), own(0, starts_col))
    count_r = jnp.where(second, own(1, count_col), own(0, count_col))
    offset_r = (((r_id >> 4) - first_r) & 31) + 32 * (r_id & 7)
    offset_r = jnp.where(offset_r < count_r, offset_r, -1)
    picked = []
    for fl in range(2):
        wanted = jnp.where(second if fl else jnp.logical_not(second), offset_r, -1)
        chosen = one_hot(iota((N_SEQ * PAIR, GRID), 1) == wanted)
        kept = one_hot(iota((GRID, GRID), 0) == keep_ref[fl : fl + 1, :])
        picked.append(dot(chosen, kept, (1, 1)).astype(BF16))
    pick = jnp.concatenate(picked, axis=1)

    def pick_heads(low, high):
        rows = [jnp.concatenate([x_ref[0, h], x_ref[1, h]], axis=0) for h in range(low, high)]
        return dot(pick, jnp.concatenate(rows, axis=1), (1, 0)).astype(BF16).reshape(N_SEQ, PAIR, -1)

    send_kv[...] = pick_heads(HEADS, HEADS + 2)

    pl.semaphore_wait(barrier, N_SEQ - 1 + N_TP - 1)

    def exchange(src, dst, at):
        @pl.loop(1, N_SEQ)
        def _(o):
            other = (me + o) & 31
            pltpu.make_async_remote_copy(
                src_ref=src.at[other],
                dst_ref=dst.at[me],
                send_sem=a2a_sem.at[at],
                recv_sem=a2a_sem.at[at + 1],
                device_id={"seq": other},
                device_id_type=MESH,
            ).start()

        key, copy = exchange_all(src, dst, at)[0]
        to_send[key] = to_recv[key] = copy

    def exchange_all(src, dst, at):
        copy = pltpu.make_async_remote_copy(
            src_ref=src.at[pl.ds(0, N_SEQ - 1)],
            dst_ref=dst.at[pl.ds(0, N_SEQ - 1)],
            send_sem=a2a_sem.at[at],
            recv_sem=a2a_sem.at[at + 1],
            device_id={"seq": (me + 1) & 31},
            device_id_type=MESH,
        )
        return [((2, 0, at), copy)]

    exchange(send_kv, recv_kv, 0)
    recv_kv[pl.ds(me, 1)] = send_kv[pl.ds(me, 1)]
    send_q[...] = pick_heads(0, HEADS)
    recv_q[pl.ds(me, 1)] = send_q[pl.ds(me, 1)]

    lane = iota((1, N_SEQ * PAIR), 1)
    at_slot = slot_col == (iota((FRAMES, N_SEQ * PAIR), 1) >> 3)
    first_l = jnp.sum(jnp.where(at_slot, starts_col, 0), axis=0, keepdims=True)
    count_l = jnp.sum(jnp.where(at_slot, count_col, 0), axis=0, keepdims=True)
    offset_l = ((me - first_l) & 31) + 32 * (lane & 7)
    row_l = jnp.where(offset_l < count_l, (first_l + offset_l) >> 5, -1)
    place = one_hot(iota((TOK, N_SEQ * PAIR), 0) == row_l)

    wait_recv(exchange_all(send_kv, recv_kv, 0))
    mine = dot(place, recv_kv[...].reshape(N_SEQ * PAIR, 2 * HD), (1, 0)).astype(BF16)
    for c in range(CHUNKS):
        kvs[c][xx, cc, zz] = mine[KEY_AT[c] : KEY_AT[c + 1], :]

    def seq_copy(c, at, src, dst, device):
        return (0, c, at), pltpu.make_async_remote_copy(
            src_ref=src, dst_ref=dst, send_sem=g_send.at[c, at], recv_sem=g_recv.at[c, at],
            device_id=device, device_id_type=MESH,
        )

    def z_all(c):
        ref = kvs[c].at[xx, cc, zz]
        return [seq_copy(c, step, ref, ref, seq_id(zz + step + 1, xx, cc)) for step in range(3)]

    def x_one(c):
        ref = kvs[c].at[xx, cc]
        steps = (1, 2, 3) if X_DIRECT else (1, 3)
        return [seq_copy(c, 2 + step, ref, ref, seq_id(zz, xx + step, cc)) for step in steps]

    def x_two(c):
        up = kvs[c].at[(xx - 1) & 3, cc, pl.ds(0, 2)]
        down = kvs[c].at[(xx + 1) & 3, cc, pl.ds(2, 2)]
        return [
            seq_copy(c, 6, up, up, seq_id(zz, xx + 1, cc)),
            seq_copy(c, 7, down, down, seq_id(zz, xx - 1, cc)),
        ]

    def sibling(c, step):
        ref = kvs[c].at[(xx + step) & 3, cc]
        return [seq_copy(c, 8 + step, ref, ref, seq_id(zz, xx, 1 - cc))]

    def gather_stage(stage, c):
        if stage == 0:
            start(z_all(c))
        elif stage == 1:
            wait_recv(z_all(c))
            start(x_one(c))
            start(sibling(c, 0))
        elif stage == 2:
            wait_recv(x_one(c))
            if not X_DIRECT:
                start(x_two(c))
            for step in (1, 3, 2) if X_DIRECT else (1, 3):
                start(sibling(c, step))
        elif stage == 3:
            if not X_DIRECT:
                wait_recv(x_two(c))
                start(sibling(c, 2))
        elif stage == 4:
            for step in range(4):
                wait_recv(sibling(c, step))

    def mark_keys():
        lanes = iota((1, HD), 1)
        firsts = jnp.sum(jnp.where(iota((FRAMES, HD), 0) < lanes, count_col, 0), axis=0, keepdims=True)
        firsts = jnp.where(lanes < FRAMES, firsts, FAR)
        q_pos = iota((TOK, 1), 0) * N_SEQ + me
        ends = jnp.min(jnp.where(firsts > q_pos, firsts, FAR), axis=1, keepdims=True)
        bias_ref[...] = jnp.where((firsts == ends) & (firsts < FAR), NEGATIVE, 0.0).astype(BF16)
        for c in range(CHUNKS):
            rows = KEY_ROWS[c]

            @pl.loop(0, N_SEQ)
            def _(i, c=c, rows=rows):
                x, core, z = i >> 3, (i >> 2) & 1, i & 3
                pos = (KEY_AT[c] + iota((rows, 1), 0)) * N_SEQ + (z * 4 + x) * 2 + core
                seen[c][pl.ds(pl.multiple_of(i * rows, 16), rows), :] = one_hot(pos >= firsts)

    def load_queries():
        wait_recv(exchange_all(send_q, recv_q, 2))
        queries = dot(place, recv_q[...].reshape(N_SEQ * PAIR, HEADS * HD), (1, 0)).astype(BF16)
        for a in range(HEADS):
            q_ref[a] = queries[:, a * HD : (a + 1) * HD]

    def attention(j, parts):
        low, high = QUERY_AT[j], QUERY_AT[j + 1]
        rows = HEADS * (high - low)
        q = jnp.concatenate(
            [q_ref[:, low:high, :].reshape(rows, HD), jnp.concatenate([bias_ref[low:high, :]] * HEADS, axis=0)], axis=1
        )
        if 0 in parts:
            m_ref[:rows] = jnp.full((rows, HD), NEGATIVE, F32)
            acc_ref[:rows] = jnp.zeros((rows, 2 * HD), F32)
        for c in parts:
            block = KEY_ROWS[c] * N_SEQ // KEY_BLOCKS[c]
            flat = kvs[c].reshape(KEY_ROWS[c] * N_SEQ, 2 * HD)

            def step(i, c=c, block=block, flat=flat):
                at = pl.multiple_of(i * block, 128)
                keys = jnp.concatenate([flat[pl.ds(at, block), :HD], seen[c][pl.ds(at, block), :]], axis=1)
                values = jnp.concatenate([flat[pl.ds(at, block), HD:], jnp.ones((block, HD), BF16)], axis=1)
                s = dot(q, keys, (1, 1))
                old = m_ref[:rows, :1]
                new = jnp.maximum(old, jnp.max(s, axis=1, keepdims=True))
                p = jnp.exp2((s - new) * SCALE).astype(BF16)
                keep = jnp.exp2((old - new) * SCALE)
                m_ref[:rows] = jnp.broadcast_to(new, (rows, HD))
                acc_ref[:rows] = acc_ref[:rows] * keep + dot(p, values, (1, 0))

            if KEY_BLOCKS[c] == 1:
                step(0)
            else:
                pl.loop(0, KEY_BLOCKS[c])(step)

        if j in parts:
            out = (acc_ref[:rows, :HD] / acc_ref[:rows, HD:]).astype(BF16)
            wide = [out[a * (high - low) : (a + 1) * (high - low)] for a in range(HEADS)]
            att_ref[: high - low] = jnp.concatenate(wide, axis=1)

    def tp_copy(u, at, src, dst, device):
        return (1, u, at), pltpu.make_async_remote_copy(
            src_ref=src, dst_ref=dst, send_sem=r_send.at[u, at], recv_sem=r_recv.at[u, at],
            device_id=device, device_id_type=MESH,
        )

    def far_halves(u):
        if PAIR_FIRST[u]:
            columns = pl.ds(0, WIDTH // 2)
            return [
                tp_copy(u, 0, half_send.at[u, 0], half_p.at[u, :, columns], tp_id(yy + 1, zl)),
                tp_copy(u, 1, half_send.at[u, 1], half_m.at[u, :, columns], tp_id(yy - 1, zl)),
            ]
        return [
            tp_copy(u, 0, part_ref.at[u, 0, y_far], half_p.at[u], tp_id(yy + 1, zl)),
            tp_copy(u, 1, part_ref.at[u, 1, y_far], half_m.at[u], tp_id(yy - 1, zl)),
        ]

    def near_blocks(u):
        if PAIR_FIRST[u]:
            return [
                tp_copy(u, 2, near_send.at[u, 0], block_p.at[u, 0], tp_id(yy + 1, zl)),
                tp_copy(u, 3, near_send.at[u, 1], block_m.at[u, 0], tp_id(yy - 1, zl)),
            ]
        return [
            tp_copy(u, 2, part_ref.at[u, :, y_up], block_p.at[u], tp_id(yy + 1, zl)),
            tp_copy(u, 3, part_ref.at[u, :, y_down], block_m.at[u], tp_id(yy - 1, zl)),
        ]

    def z_pair(u):
        return [tp_copy(u, 4, z_send.at[u], z_recv.at[u], tp_id(yy, 1 - zl))]

    def z_piece(u, step):
        y = (yy + step) & 3
        return [tp_copy(u, 4 + step, part_ref.at[u, 1 - zl, y], pair_ref.at[u, y], tp_id(yy, 1 - zl))]

    def project(j):
        low, high = QUERY_AT[j], QUERY_AT[j + 1]
        for step in (2, 1, 3, 0):
            y = (yy + step) & 3
            w = w_ref[:, pl.ds(pl.multiple_of(y * 2 * WIDTH, 2 * WIDTH), 2 * WIDTH)]
            out = dot(att_ref[: high - low], w, (1, 0)).astype(BF16)
            for n, u in enumerate(UNITS_OF[j]):
                part_ref[u, 0, y] = out[n * UNIT : (n + 1) * UNIT, :WIDTH]
                part_ref[u, 1, y] = out[n * UNIT : (n + 1) * UNIT, WIDTH:]
            for u in UNITS_OF[j]:
                if PAIR_FIRST[u]:
                    start(z_piece(u, step))
                elif step == 2:
                    start(far_halves(u))

    def paired(u, y):
        return part_ref[u, zl, y].astype(F32) + pair_ref[u, y].astype(F32)

    def reduce_pair(u):
        wait_recv(z_piece(u, 2))
        both = paired(u, y_far).astype(BF16)
        half_send[u, 0] = both[:, : WIDTH // 2]
        half_send[u, 1] = both[:, WIDTH // 2 :]
        start(far_halves(u))

    def reduce_near(u):
        if PAIR_FIRST[u]:
            half = WIDTH // 2
            wait_recv(z_piece(u, 1) + z_piece(u, 3) + far_halves(u))
            up, down = paired(u, y_up), paired(u, y_down)
            near_send[u, 0, :, :half] = (up[:, :half] + half_p[u, :, :half].astype(F32)).astype(BF16)
            near_send[u, 0, :, half:] = up[:, half:].astype(BF16)
            near_send[u, 1, :, :half] = down[:, :half].astype(BF16)
            near_send[u, 1, :, half:] = (down[:, half:] + half_m[u, :, :half].astype(F32)).astype(BF16)
        else:
            wait_recv(far_halves(u))
            part_ref[u, 0, y_up] = (part_ref[u, 0, y_up].astype(F32) + half_p[u].astype(F32)).astype(BF16)
            part_ref[u, 1, y_down] = (part_ref[u, 1, y_down].astype(F32) + half_m[u].astype(F32)).astype(BF16)
        start(near_blocks(u))

    def reduce_own(u):
        wait_recv(near_blocks(u))
        rows = pl.ds(u * UNIT, UNIT)

        def total(h):
            return part_ref[u, h, yy].astype(F32) + block_p[u, h].astype(F32) + block_m[u, h].astype(F32)

        if PAIR_FIRST[u]:
            wait_recv(z_piece(u, 0))
            finish(rows, paired(u, yy) + block_p[u, 0].astype(F32) + block_m[u, 0].astype(F32) + res_ref[rows, :].astype(F32))
        else:
            z_send[u] = total(1 - zl).astype(BF16)
            start(z_pair(u))
            stream_ref[rows, :] = total(zl) + res_ref[rows, :].astype(F32)

    def finish(rows, stream):
        stream_ref[rows, :] = stream
        ssq_ref[rows, :] = jnp.broadcast_to(jnp.sum(stream * stream, axis=1, keepdims=True), (UNIT, HD))

    def finish_rows(u):
        if not PAIR_FIRST[u]:
            wait_recv(z_pair(u))
            rows = pl.ds(u * UNIT, UNIT)
            finish(rows, stream_ref[rows, :] + z_recv[u].astype(F32))

    gather_stage(0, 0)
    gather_stage(0, 1)
    gather_stage(0, 2)
    gather_stage(0, 3)
    gather_stage(1, 0)
    gather_stage(1, 1)
    exchange(send_q, recv_q, 2)
    mark_keys()
    gather_stage(1, 2)
    gather_stage(1, 3)
    gather_stage(2, 0)
    gather_stage(2, 1)
    gather_stage(2, 2)
    gather_stage(2, 3)
    gather_stage(3, 0)
    gather_stage(3, 1)
    gather_stage(3, 2)
    gather_stage(3, 3)
    load_queries()
    gather_stage(4, 0)
    attention(0, (0,))
    w_copy.wait()
    project(0)
    gather_stage(4, 1)
    attention(1, (0, 1))
    reduce_pair(1)
    reduce_near(0)
    project(1)
    gather_stage(4, 2)
    attention(2, (0, 1, 2))
    reduce_pair(3)
    reduce_near(2)
    reduce_near(1)
    reduce_own(0)
    project(2)
    gather_stage(4, 3)
    attention(3, (0, 1, 2, 3))
    reduce_pair(5)
    reduce_near(4)
    reduce_near(3)
    reduce_own(2)
    reduce_own(1)
    finish_rows(0)
    project(3)
    reduce_pair(7)
    reduce_near(6)
    reduce_near(5)
    reduce_own(4)
    reduce_own(3)
    finish_rows(2)
    reduce_near(7)
    reduce_own(6)
    reduce_own(5)
    finish_rows(4)
    reduce_own(7)
    finish_rows(6)

    diag = iota((TOK, TOK), 0) == iota((TOK, TOK), 1)
    ssq_row = jnp.sum(jnp.where(diag, ssq_ref[:, :1], 0.0), axis=0, keepdims=True)
    ssq_send[...] = jnp.broadcast_to(ssq_row, (8, TOK))
    ssq_recv[pl.ds(tp, 1)] = ssq_send[...][None]

    @pl.loop(1, N_TP)
    def _(o):
        pltpu.make_async_remote_copy(
            src_ref=ssq_send, dst_ref=ssq_recv.at[tp], send_sem=s_sem.at[0], recv_sem=s_sem.at[1],
            device_id={"tp": (tp + o) & 7}, device_id_type=MESH,
        ).start()

    ssq_all = pltpu.make_async_remote_copy(
        src_ref=ssq_recv.at[pl.ds(0, N_TP - 1)], dst_ref=ssq_recv.at[pl.ds(0, N_TP - 1)],
        send_sem=s_sem.at[0], recv_sem=s_sem.at[1],
        device_id={"tp": (tp + 1) & 7}, device_id_type=MESH,
    )
    for key in to_send:
        to_send[key].wait_send()
    ssq_all.wait_recv()
    sums = jnp.sum(ssq_recv[...], axis=0)[:1, :]
    inverse_row = lax.rsqrt(sums / D + EPSILON)
    inverse = jnp.sum(jnp.where(diag, inverse_row, 0.0), axis=1, keepdims=True)
    inverse_ref[...] = jnp.broadcast_to(inverse, (TOK, HD))
    ssq_all.wait_send()


def normalize(stream_ref, inverse_ref, gain_ref, hid_ref, nrm_ref):
    stream = stream_ref[...]
    gain = gain_ref[...].astype(F32).reshape(1, WIDTH)
    hid_ref[...] = stream.astype(BF16)
    nrm_ref[...] = (stream * inverse_ref[:, :1] * gain).astype(BF16)


def body(frame_grid, keep_rows, kept_count, frame_slot, out_weight, residual, norm_gain):
    vmem = pl.BlockSpec(memory_space=pltpu.VMEM)
    dma = pltpu.SemaphoreType.DMA
    stream, inverse = pl.pallas_call(
        kernel,
        out_shape=[jax.ShapeDtypeStruct((TOK, WIDTH), F32), jax.ShapeDtypeStruct((TOK, HD), F32)],
        in_specs=[vmem] * 4 + [pl.BlockSpec(memory_space=pl.ANY)] + [vmem],
        out_specs=[vmem] * 2,
        scratch_shapes=[
            pltpu.VMEM((N_SEQ, PAIR, 2 * HD), BF16),
            pltpu.VMEM((N_SEQ, PAIR, HEADS * HD), BF16),
            pltpu.VMEM((N_SEQ, PAIR, 2 * HD), BF16),
            pltpu.VMEM((N_SEQ, PAIR, HEADS * HD), BF16),
        ]
        + [pltpu.VMEM((4, 2, 4, rows, 2 * HD), BF16) for rows in KEY_ROWS]
        + [pltpu.VMEM((N_SEQ * rows, HD), BF16) for rows in KEY_ROWS]
        + [
            pltpu.VMEM((HEADS, TOK, HD), BF16),
            pltpu.VMEM((TOK, HD), BF16),
            pltpu.VMEM((HEADS * HD, D), BF16),
            pltpu.VMEM((HEADS * MOST, HD), F32),
            pltpu.VMEM((HEADS * MOST, 2 * HD), F32),
            pltpu.VMEM((MOST, HEADS * HD), BF16),
            pltpu.VMEM((UNITS, 2, 4, UNIT, WIDTH), BF16),
            pltpu.VMEM((UNITS, 4, UNIT, WIDTH), BF16),
            pltpu.VMEM((UNITS, 2, UNIT, WIDTH // 2), BF16),
            pltpu.VMEM((UNITS, UNIT, WIDTH), BF16),
            pltpu.VMEM((UNITS, UNIT, WIDTH), BF16),
            pltpu.VMEM((UNITS, 2, UNIT, WIDTH), BF16),
            pltpu.VMEM((UNITS, 2, UNIT, WIDTH), BF16),
            pltpu.VMEM((UNITS, 2, UNIT, WIDTH), BF16),
            pltpu.VMEM((UNITS, UNIT, WIDTH), BF16),
            pltpu.VMEM((UNITS, UNIT, WIDTH), BF16),
            pltpu.VMEM((TOK, HD), F32),
            pltpu.VMEM((8, TOK), F32),
            pltpu.VMEM((N_TP, 8, TOK), F32),
            dma((4,)),
            dma((CHUNKS, 12)),
            dma((CHUNKS, 12)),
            dma((UNITS, 8)),
            dma((UNITS, 8)),
            dma((2,)),
            dma,
        ],
        compiler_params=pltpu.CompilerParams(
            collective_id=0, has_side_effects=True, vmem_limit_bytes=56 * 1024 * 1024
        ),
        cost_estimate=pl.CostEstimate(flops=5 * 10**9, bytes_accessed=12 * 10**6, transcendentals=5 * 10**6),
    )(
        frame_grid[:, :, 0].transpose(0, 2, 1, 3),
        keep_rows,
        kept_count.reshape(1, FRAMES),
        frame_slot.reshape(1, FRAMES),
        out_weight,
        residual,
    )
    return pl.pallas_call(
        normalize,
        out_shape=[jax.ShapeDtypeStruct((TOK, WIDTH), BF16)] * 2,
        in_specs=[vmem] * 3,
        out_specs=[vmem] * 2,
        cost_estimate=pl.CostEstimate(flops=10**6, bytes_accessed=2 * 10**6, transcendentals=0),
    )(stream, inverse, norm_gain)


def solution(mesh):
    in_specs = (
        P("seq", None, "tp", None, None),
        P("seq", None),
        P(),
        P(),
        P("tp", None),
        P("seq", "tp"),
        P("tp"),
    )
    out_specs = (P("seq", "tp"), P("seq", "tp"))
    return jax.shard_map(body, mesh=mesh, in_specs=in_specs, out_specs=out_specs, check_vma=False)
```

```python
import math

import jax
import jax.numpy as jnp
from jax import lax
from jax.experimental import pallas as pl
from jax.experimental.pallas import tpu as pltpu
from jax.sharding import PartitionSpec as P

D = 8192
HD = 128
HEADS = 4
FRAMES = 64
GRID = 256
TOK = 256
N_SEQ = 32
N_TP = 8
WIDTH = D // N_TP
PAIR = 16
QUERY_AT = (0, 64, 128, 192, 256)
KEY_AT = (0, 80, 144, 208, 256)
CHUNKS = 4
KEY_ROWS = tuple(KEY_AT[i + 1] - KEY_AT[i] for i in range(CHUNKS))
KEY_BLOCKS = (1, 1, 1, 1)
MOST = max(QUERY_AT[i + 1] - QUERY_AT[i] for i in range(CHUNKS))
UNIT = 32
UNITS = TOK // UNIT
PAIR_FIRST = (False, True, False, True, False, True, False, True)
UNITS_OF = ((0, 1), (2, 3), (4, 5), (6, 7))
X_DIRECT = False
NEGATIVE = -1e30
FAR = 1 << 20
EPSILON = 1e-06
SCALE = math.log2(math.e) / math.sqrt(HD)
MESH = pl.DeviceIdType.MESH
F32 = jnp.float32
BF16 = jnp.bfloat16


def iota(shape, dim):
    return lax.broadcasted_iota(jnp.int32, shape, dim)


def one_hot(mask):
    return jnp.where(mask, 1.0, 0.0).astype(BF16)


def dot(a, b, contract):
    return lax.dot_general(a, b, ((contract[:1], contract[1:]), ((), ())), preferred_element_type=F32)


def kernel(
    x_ref, keep_ref, count_ref, slot_ref, w_hbm, res_ref,
    stream_ref, inverse_ref,
    send_kv, send_q, recv_kv, recv_q, kv0, kv1, kv2, kv3, seen0, seen1, seen2, seen3, q_ref, bias_ref, w_ref,
    m_ref, acc_ref, att_ref, part_ref, pair_ref, half_send, half_p, half_m, near_send, block_p, block_m,
    z_send, z_recv, ssq_ref, ssq_send, ssq_recv,
    a2a_sem, g_send, g_recv, r_send, r_recv, s_sem, w_sem,
):
    kvs, seen = (kv0, kv1, kv2, kv3), (seen0, seen1, seen2, seen3)
    me = lax.axis_index("seq")
    tp = lax.axis_index("tp")
    zz, xx, cc = me >> 3, (me >> 1) & 3, me & 1
    yy, zl = tp >> 1, tp & 1
    y_up, y_down, y_far = (yy + 1) & 3, (yy - 1) & 3, (yy + 2) & 3

    def seq_id(z, x, c):
        return {"seq": (((z & 3) * 4 + (x & 3)) * 2 + c)}

    def tp_id(y, z):
        return {"tp": (y & 3) * 2 + z}

    to_send, to_recv = {}, {}

    def start(copies):
        for key, copy in copies:
            copy.start()
            to_send[key] = to_recv[key] = copy

    def wait_recv(copies):
        for key, copy in copies:
            copy.wait_recv()
            to_recv.pop(key)

    w_copy = pltpu.make_async_copy(w_hbm, w_ref, w_sem)
    w_copy.start()

    barrier = pltpu.get_barrier_semaphore()

    @pl.loop(1, N_SEQ)
    def _(o):
        pl.semaphore_signal(barrier, inc=1, device_id={"seq": (me + o) & 31}, device_id_type=MESH)

    @pl.loop(1, N_TP)
    def _(o):
        pl.semaphore_signal(barrier, inc=1, device_id={"tp": (tp + o) & 7}, device_id_type=MESH)

    f_col, f_row = iota((FRAMES, FRAMES), 0), iota((FRAMES, FRAMES), 1)
    counts, slots = count_ref[...], slot_ref[...]
    starts_col = jnp.sum(jnp.where(f_row < f_col, counts, 0), axis=1, keepdims=True)
    count_col = jnp.sum(jnp.where(f_row == f_col, counts, 0), axis=1, keepdims=True)
    slot_col = jnp.sum(jnp.where(f_row == f_col, slots, 0), axis=1, keepdims=True)

    r_id = iota((N_SEQ * PAIR, 1), 0)
    second = ((r_id >> 3) & 1) == 1

    def own(fl, values):
        return jnp.sum(jnp.where(slot_col == 2 * me + fl, values, 0), axis=0, keepdims=True)

    first_r = jnp.where(second, own(1, starts_col), own(0, starts_col))
    count_r = jnp.where(second, own(1, count_col), own(0, count_col))
    offset_r = (((r_id >> 4) - first_r) & 31) + 32 * (r_id & 7)
    offset_r = jnp.where(offset_r < count_r, offset_r, -1)
    picked = []
    for fl in range(2):
        wanted = jnp.where(second if fl else jnp.logical_not(second), offset_r, -1)
        chosen = one_hot(iota((N_SEQ * PAIR, GRID), 1) == wanted)
        kept = one_hot(iota((GRID, GRID), 0) == keep_ref[fl : fl + 1, :])
        picked.append(dot(chosen, kept, (1, 1)).astype(BF16))
    pick = jnp.concatenate(picked, axis=1)

    def pick_heads(low, high):
        rows = [jnp.concatenate([x_ref[0, h], x_ref[1, h]], axis=0) for h in range(low, high)]
        return dot(pick, jnp.concatenate(rows, axis=1), (1, 0)).astype(BF16).reshape(N_SEQ, PAIR, -1)

    send_kv[...] = pick_heads(HEADS, HEADS + 2)

    pl.semaphore_wait(barrier, N_SEQ - 1 + N_TP - 1)

    def exchange(src, dst, at):
        @pl.loop(1, N_SEQ)
        def _(o):
            other = (me + o) & 31
            pltpu.make_async_remote_copy(
                src_ref=src.at[other],
                dst_ref=dst.at[me],
                send_sem=a2a_sem.at[at],
                recv_sem=a2a_sem.at[at + 1],
                device_id={"seq": other},
                device_id_type=MESH,
            ).start()

        key, copy = exchange_all(src, dst, at)[0]
        to_send[key] = to_recv[key] = copy

    def exchange_all(src, dst, at):
        copy = pltpu.make_async_remote_copy(
            src_ref=src.at[pl.ds(0, N_SEQ - 1)],
            dst_ref=dst.at[pl.ds(0, N_SEQ - 1)],
            send_sem=a2a_sem.at[at],
            recv_sem=a2a_sem.at[at + 1],
            device_id={"seq": (me + 1) & 31},
            device_id_type=MESH,
        )
        return [((2, 0, at), copy)]

    exchange(send_kv, recv_kv, 0)
    recv_kv[pl.ds(me, 1)] = send_kv[pl.ds(me, 1)]
    send_q[...] = pick_heads(0, HEADS)
    recv_q[pl.ds(me, 1)] = send_q[pl.ds(me, 1)]

    lane = iota((1, N_SEQ * PAIR), 1)
    at_slot = slot_col == (iota((FRAMES, N_SEQ * PAIR), 1) >> 3)
    first_l = jnp.sum(jnp.where(at_slot, starts_col, 0), axis=0, keepdims=True)
    count_l = jnp.sum(jnp.where(at_slot, count_col, 0), axis=0, keepdims=True)
    offset_l = ((me - first_l) & 31) + 32 * (lane & 7)
    row_l = jnp.where(offset_l < count_l, (first_l + offset_l) >> 5, -1)
    place = one_hot(iota((TOK, N_SEQ * PAIR), 0) == row_l)

    wait_recv(exchange_all(send_kv, recv_kv, 0))
    mine = dot(place, recv_kv[...].reshape(N_SEQ * PAIR, 2 * HD), (1, 0)).astype(BF16)
    for c in range(CHUNKS):
        kvs[c][xx, cc, zz] = mine[KEY_AT[c] : KEY_AT[c + 1], :]

    def seq_copy(c, at, src, dst, device):
        return (0, c, at), pltpu.make_async_remote_copy(
            src_ref=src, dst_ref=dst, send_sem=g_send.at[c, at], recv_sem=g_recv.at[c, at],
            device_id=device, device_id_type=MESH,
        )

    def z_all(c):
        ref = kvs[c].at[xx, cc, zz]
        return [seq_copy(c, step, ref, ref, seq_id(zz + step + 1, xx, cc)) for step in range(3)]

    def x_one(c):
        ref = kvs[c].at[xx, cc]
        steps = (1, 2, 3) if X_DIRECT else (1, 3)
        return [seq_copy(c, 2 + step, ref, ref, seq_id(zz, xx + step, cc)) for step in steps]

    def x_two(c):
        up = kvs[c].at[(xx - 1) & 3, cc, pl.ds(0, 2)]
        down = kvs[c].at[(xx + 1) & 3, cc, pl.ds(2, 2)]
        return [
            seq_copy(c, 6, up, up, seq_id(zz, xx + 1, cc)),
            seq_copy(c, 7, down, down, seq_id(zz, xx - 1, cc)),
        ]

    def sibling(c, step):
        ref = kvs[c].at[(xx + step) & 3, cc]
        return [seq_copy(c, 8 + step, ref, ref, seq_id(zz, xx, 1 - cc))]

    def gather_stage(stage, c):
        if stage == 0:
            start(z_all(c))
        elif stage == 1:
            wait_recv(z_all(c))
            start(x_one(c))
            start(sibling(c, 0))
        elif stage == 2:
            wait_recv(x_one(c))
            if not X_DIRECT:
                start(x_two(c))
            for step in (1, 3, 2) if X_DIRECT else (1, 3):
                start(sibling(c, step))
        elif stage == 3:
            if not X_DIRECT:
                wait_recv(x_two(c))
                start(sibling(c, 2))
        elif stage == 4:
            for step in range(4):
                wait_recv(sibling(c, step))

    def mark_keys():
        lanes = iota((1, HD), 1)
        firsts = jnp.sum(jnp.where(iota((FRAMES, HD), 0) < lanes, count_col, 0), axis=0, keepdims=True)
        firsts = jnp.where(lanes < FRAMES, firsts, FAR)
        q_pos = iota((TOK, 1), 0) * N_SEQ + me
        ends = jnp.min(jnp.where(firsts > q_pos, firsts, FAR), axis=1, keepdims=True)
        bias_ref[...] = jnp.where((firsts == ends) & (firsts < FAR), NEGATIVE, 0.0).astype(BF16)
        for c in range(CHUNKS):
            rows = KEY_ROWS[c]

            @pl.loop(0, N_SEQ)
            def _(i, c=c, rows=rows):
                x, core, z = i >> 3, (i >> 2) & 1, i & 3
                pos = (KEY_AT[c] + iota((rows, 1), 0)) * N_SEQ + (z * 4 + x) * 2 + core
                seen[c][pl.ds(pl.multiple_of(i * rows, 16), rows), :] = one_hot(pos >= firsts)

    def load_queries():
        wait_recv(exchange_all(send_q, recv_q, 2))
        queries = dot(place, recv_q[...].reshape(N_SEQ * PAIR, HEADS * HD), (1, 0)).astype(BF16)
        for a in range(HEADS):
            q_ref[a] = queries[:, a * HD : (a + 1) * HD]

    def attention(j, parts):
        low, high = QUERY_AT[j], QUERY_AT[j + 1]
        rows = HEADS * (high - low)
        q = jnp.concatenate(
            [q_ref[:, low:high, :].reshape(rows, HD), jnp.concatenate([bias_ref[low:high, :]] * HEADS, axis=0)], axis=1
        )
        if 0 in parts:
            m_ref[:rows] = jnp.full((rows, HD), NEGATIVE, F32)
            acc_ref[:rows] = jnp.zeros((rows, 2 * HD), F32)
        for c in parts:
            block = KEY_ROWS[c] * N_SEQ // KEY_BLOCKS[c]
            flat = kvs[c].reshape(KEY_ROWS[c] * N_SEQ, 2 * HD)

            def step(i, c=c, block=block, flat=flat):
                at = pl.multiple_of(i * block, 128)
                keys = jnp.concatenate([flat[pl.ds(at, block), :HD], seen[c][pl.ds(at, block), :]], axis=1)
                values = jnp.concatenate([flat[pl.ds(at, block), HD:], jnp.ones((block, HD), BF16)], axis=1)
                s = dot(q, keys, (1, 1))
                old = m_ref[:rows, :1]
                new = jnp.maximum(old, jnp.max(s, axis=1, keepdims=True))
                p = jnp.exp2((s - new) * SCALE).astype(BF16)
                keep = jnp.exp2((old - new) * SCALE)
                m_ref[:rows] = jnp.broadcast_to(new, (rows, HD))
                acc_ref[:rows] = acc_ref[:rows] * keep + dot(p, values, (1, 0))

            if KEY_BLOCKS[c] == 1:
                step(0)
            else:
                pl.loop(0, KEY_BLOCKS[c])(step)

        if j in parts:
            out = (acc_ref[:rows, :HD] / acc_ref[:rows, HD:]).astype(BF16)
            wide = [out[a * (high - low) : (a + 1) * (high - low)] for a in range(HEADS)]
            att_ref[: high - low] = jnp.concatenate(wide, axis=1)

    def tp_copy(u, at, src, dst, device):
        return (1, u, at), pltpu.make_async_remote_copy(
            src_ref=src, dst_ref=dst, send_sem=r_send.at[u, at], recv_sem=r_recv.at[u, at],
            device_id=device, device_id_type=MESH,
        )

    def far_halves(u):
        if PAIR_FIRST[u]:
            columns = pl.ds(0, WIDTH // 2)
            return [
                tp_copy(u, 0, half_send.at[u, 0], half_p.at[u, :, columns], tp_id(yy + 1, zl)),
                tp_copy(u, 1, half_send.at[u, 1], half_m.at[u, :, columns], tp_id(yy - 1, zl)),
            ]
        return [
            tp_copy(u, 0, part_ref.at[u, 0, y_far], half_p.at[u], tp_id(yy + 1, zl)),
            tp_copy(u, 1, part_ref.at[u, 1, y_far], half_m.at[u], tp_id(yy - 1, zl)),
        ]

    def near_blocks(u):
        if PAIR_FIRST[u]:
            return [
                tp_copy(u, 2, near_send.at[u, 0], block_p.at[u, 0], tp_id(yy + 1, zl)),
                tp_copy(u, 3, near_send.at[u, 1], block_m.at[u, 0], tp_id(yy - 1, zl)),
            ]
        return [
            tp_copy(u, 2, part_ref.at[u, :, y_up], block_p.at[u], tp_id(yy + 1, zl)),
            tp_copy(u, 3, part_ref.at[u, :, y_down], block_m.at[u], tp_id(yy - 1, zl)),
        ]

    def z_pair(u):
        return [tp_copy(u, 4, z_send.at[u], z_recv.at[u], tp_id(yy, 1 - zl))]

    def z_piece(u, step):
        y = (yy + step) & 3
        return [tp_copy(u, 4 + step, part_ref.at[u, 1 - zl, y], pair_ref.at[u, y], tp_id(yy, 1 - zl))]

    def project(j):
        low, high = QUERY_AT[j], QUERY_AT[j + 1]
        for step in (2, 1, 3, 0):
            y = (yy + step) & 3
            w = w_ref[:, pl.ds(pl.multiple_of(y * 2 * WIDTH, 2 * WIDTH), 2 * WIDTH)]
            out = dot(att_ref[: high - low], w, (1, 0)).astype(BF16)
            for n, u in enumerate(UNITS_OF[j]):
                part_ref[u, 0, y] = out[n * UNIT : (n + 1) * UNIT, :WIDTH]
                part_ref[u, 1, y] = out[n * UNIT : (n + 1) * UNIT, WIDTH:]
            for u in UNITS_OF[j]:
                if PAIR_FIRST[u]:
                    start(z_piece(u, step))
                elif step == 2:
                    start(far_halves(u))

    def paired(u, y):
        return part_ref[u, zl, y].astype(F32) + pair_ref[u, y].astype(F32)

    def reduce_pair(u):
        wait_recv(z_piece(u, 2))
        both = paired(u, y_far).astype(BF16)
        half_send[u, 0] = both[:, : WIDTH // 2]
        half_send[u, 1] = both[:, WIDTH // 2 :]
        start(far_halves(u))

    def reduce_near(u):
        if PAIR_FIRST[u]:
            half = WIDTH // 2
            wait_recv(z_piece(u, 1) + z_piece(u, 3) + far_halves(u))
            up, down = paired(u, y_up), paired(u, y_down)
            near_send[u, 0, :, :half] = (up[:, :half] + half_p[u, :, :half].astype(F32)).astype(BF16)
            near_send[u, 0, :, half:] = up[:, half:].astype(BF16)
            near_send[u, 1, :, :half] = down[:, :half].astype(BF16)
            near_send[u, 1, :, half:] = (down[:, half:] + half_m[u, :, :half].astype(F32)).astype(BF16)
        else:
            wait_recv(far_halves(u))
            part_ref[u, 0, y_up] = (part_ref[u, 0, y_up].astype(F32) + half_p[u].astype(F32)).astype(BF16)
            part_ref[u, 1, y_down] = (part_ref[u, 1, y_down].astype(F32) + half_m[u].astype(F32)).astype(BF16)
        start(near_blocks(u))

    def reduce_own(u):
        wait_recv(near_blocks(u))
        rows = pl.ds(u * UNIT, UNIT)

        def total(h):
            return part_ref[u, h, yy].astype(F32) + block_p[u, h].astype(F32) + block_m[u, h].astype(F32)

        if PAIR_FIRST[u]:
            wait_recv(z_piece(u, 0))
            finish(rows, paired(u, yy) + block_p[u, 0].astype(F32) + block_m[u, 0].astype(F32) + res_ref[rows, :].astype(F32))
        else:
            z_send[u] = total(1 - zl).astype(BF16)
            start(z_pair(u))
            stream_ref[rows, :] = total(zl) + res_ref[rows, :].astype(F32)

    def finish(rows, stream):
        stream_ref[rows, :] = stream
        ssq_ref[rows, :] = jnp.broadcast_to(jnp.sum(stream * stream, axis=1, keepdims=True), (UNIT, HD))

    def finish_rows(u):
        if not PAIR_FIRST[u]:
            wait_recv(z_pair(u))
            rows = pl.ds(u * UNIT, UNIT)
            finish(rows, stream_ref[rows, :] + z_recv[u].astype(F32))

    gather_stage(0, 0)
    gather_stage(0, 2)
    gather_stage(0, 1)
    gather_stage(1, 0)
    exchange(send_q, recv_q, 2)
    gather_stage(1, 2)
    mark_keys()
    gather_stage(2, 0)
    gather_stage(1, 1)
    gather_stage(2, 2)
    gather_stage(0, 3)
    gather_stage(3, 0)
    load_queries()
    gather_stage(4, 0)
    attention(0, (0,))
    gather_stage(2, 1)
    w_copy.wait()
    project(0)
    gather_stage(3, 2)
    gather_stage(1, 3)
    gather_stage(3, 1)
    gather_stage(4, 2)
    reduce_near(0)
    gather_stage(4, 1)
    reduce_pair(1)
    attention(1, (0, 1))
    gather_stage(2, 3)
    project(1)
    attention(2, (0, 1, 2))
    gather_stage(3, 3)
    reduce_near(1)
    reduce_own(0)
    project(2)
    gather_stage(4, 3)
    reduce_near(2)
    reduce_pair(3)
    attention(3, (0, 1, 2, 3))
    reduce_near(4)
    reduce_own(1)
    finish_rows(0)
    project(3)
    reduce_pair(5)
    reduce_own(2)
    reduce_near(3)
    reduce_own(4)
    reduce_pair(7)
    reduce_near(6)
    reduce_near(5)
    reduce_own(3)
    reduce_near(7)
    finish_rows(2)
    reduce_own(6)
    finish_rows(4)
    reduce_own(5)
    reduce_own(7)
    finish_rows(6)

    diag = iota((TOK, TOK), 0) == iota((TOK, TOK), 1)
    ssq_row = jnp.sum(jnp.where(diag, ssq_ref[:, :1], 0.0), axis=0, keepdims=True)
    ssq_send[...] = jnp.broadcast_to(ssq_row, (8, TOK))
    ssq_recv[pl.ds(tp, 1)] = ssq_send[...][None]

    @pl.loop(1, N_TP)
    def _(o):
        pltpu.make_async_remote_copy(
            src_ref=ssq_send, dst_ref=ssq_recv.at[tp], send_sem=s_sem.at[0], recv_sem=s_sem.at[1],
            device_id={"tp": (tp + o) & 7}, device_id_type=MESH,
        ).start()

    ssq_all = pltpu.make_async_remote_copy(
        src_ref=ssq_recv.at[pl.ds(0, N_TP - 1)], dst_ref=ssq_recv.at[pl.ds(0, N_TP - 1)],
        send_sem=s_sem.at[0], recv_sem=s_sem.at[1],
        device_id={"tp": (tp + 1) & 7}, device_id_type=MESH,
    )
    for key in to_send:
        to_send[key].wait_send()
    ssq_all.wait_recv()
    sums = jnp.sum(ssq_recv[...], axis=0)[:1, :]
    inverse_row = lax.rsqrt(sums / D + EPSILON)
    inverse = jnp.sum(jnp.where(diag, inverse_row, 0.0), axis=1, keepdims=True)
    inverse_ref[...] = jnp.broadcast_to(inverse, (TOK, HD))
    ssq_all.wait_send()


def normalize(stream_ref, inverse_ref, gain_ref, hid_ref, nrm_ref):
    stream = stream_ref[...]
    gain = gain_ref[...].astype(F32).reshape(1, WIDTH)
    hid_ref[...] = stream.astype(BF16)
    nrm_ref[...] = (stream * inverse_ref[:, :1] * gain).astype(BF16)


def body(frame_grid, keep_rows, kept_count, frame_slot, out_weight, residual, norm_gain):
    vmem = pl.BlockSpec(memory_space=pltpu.VMEM)
    dma = pltpu.SemaphoreType.DMA
    stream, inverse = pl.pallas_call(
        kernel,
        out_shape=[jax.ShapeDtypeStruct((TOK, WIDTH), F32), jax.ShapeDtypeStruct((TOK, HD), F32)],
        in_specs=[vmem] * 4 + [pl.BlockSpec(memory_space=pl.ANY)] + [vmem],
        out_specs=[vmem] * 2,
        scratch_shapes=[
            pltpu.VMEM((N_SEQ, PAIR, 2 * HD), BF16),
            pltpu.VMEM((N_SEQ, PAIR, HEADS * HD), BF16),
            pltpu.VMEM((N_SEQ, PAIR, 2 * HD), BF16),
            pltpu.VMEM((N_SEQ, PAIR, HEADS * HD), BF16),
        ]
        + [pltpu.VMEM((4, 2, 4, rows, 2 * HD), BF16) for rows in KEY_ROWS]
        + [pltpu.VMEM((N_SEQ * rows, HD), BF16) for rows in KEY_ROWS]
        + [
            pltpu.VMEM((HEADS, TOK, HD), BF16),
            pltpu.VMEM((TOK, HD), BF16),
            pltpu.VMEM((HEADS * HD, D), BF16),
            pltpu.VMEM((HEADS * MOST, HD), F32),
            pltpu.VMEM((HEADS * MOST, 2 * HD), F32),
            pltpu.VMEM((MOST, HEADS * HD), BF16),
            pltpu.VMEM((UNITS, 2, 4, UNIT, WIDTH), BF16),
            pltpu.VMEM((UNITS, 4, UNIT, WIDTH), BF16),
            pltpu.VMEM((UNITS, 2, UNIT, WIDTH // 2), BF16),
            pltpu.VMEM((UNITS, UNIT, WIDTH), BF16),
            pltpu.VMEM((UNITS, UNIT, WIDTH), BF16),
            pltpu.VMEM((UNITS, 2, UNIT, WIDTH), BF16),
            pltpu.VMEM((UNITS, 2, UNIT, WIDTH), BF16),
            pltpu.VMEM((UNITS, 2, UNIT, WIDTH), BF16),
            pltpu.VMEM((UNITS, UNIT, WIDTH), BF16),
            pltpu.VMEM((UNITS, UNIT, WIDTH), BF16),
            pltpu.VMEM((TOK, HD), F32),
            pltpu.VMEM((8, TOK), F32),
            pltpu.VMEM((N_TP, 8, TOK), F32),
            dma((4,)),
            dma((CHUNKS, 12)),
            dma((CHUNKS, 12)),
            dma((UNITS, 8)),
            dma((UNITS, 8)),
            dma((2,)),
            dma,
        ],
        compiler_params=pltpu.CompilerParams(
            collective_id=0, has_side_effects=True, vmem_limit_bytes=56 * 1024 * 1024
        ),
        cost_estimate=pl.CostEstimate(flops=5 * 10**9, bytes_accessed=12 * 10**6, transcendentals=5 * 10**6),
    )(
        frame_grid[:, :, 0].transpose(0, 2, 1, 3),
        keep_rows,
        kept_count.reshape(1, FRAMES),
        frame_slot.reshape(1, FRAMES),
        out_weight,
        residual,
    )
    return pl.pallas_call(
        normalize,
        out_shape=[jax.ShapeDtypeStruct((TOK, WIDTH), BF16)] * 2,
        in_specs=[vmem] * 3,
        out_specs=[vmem] * 2,
        cost_estimate=pl.CostEstimate(flops=10**6, bytes_accessed=2 * 10**6, transcendentals=0),
    )(stream, inverse, norm_gain)


def solution(mesh):
    in_specs = (
        P("seq", None, "tp", None, None),
        P("seq", None),
        P(),
        P(),
        P("tp", None),
        P("seq", "tp"),
        P("tp"),
    )
    out_specs = (P("seq", "tp"), P("seq", "tp"))
    return jax.shard_map(body, mesh=mesh, in_specs=in_specs, out_specs=out_specs, check_vma=False)
```

```python
import math

import jax
import jax.numpy as jnp
from jax import lax
from jax.experimental import pallas as pl
from jax.experimental.pallas import tpu as pltpu
from jax.sharding import PartitionSpec as P

D = 8192
HD = 128
HEADS = 4
FRAMES = 64
GRID = 256
TOK = 256
N_SEQ = 32
N_TP = 8
WIDTH = D // N_TP
PAIR = 16
QUERY_AT = (0, 64, 128, 192, 256)
KEY_AT = (0, 80, 144, 208, 256)
CHUNKS = 4
KEY_ROWS = tuple(KEY_AT[i + 1] - KEY_AT[i] for i in range(CHUNKS))
KEY_BLOCKS = (1, 1, 1, 1)
MOST = max(QUERY_AT[i + 1] - QUERY_AT[i] for i in range(CHUNKS))
UNIT = 32
UNITS = TOK // UNIT
PAIR_FIRST = (False, True, False, True, False, True, False, True)
UNITS_OF = ((0, 1), (2, 3), (4, 5), (6, 7))
Z_DIRECT = (0, 1, 2, 3)
NEGATIVE = -1e30
FAR = 1 << 20
EPSILON = 1e-06
SCALE = math.log2(math.e) / math.sqrt(HD)
MESH = pl.DeviceIdType.MESH
F32 = jnp.float32
BF16 = jnp.bfloat16


def iota(shape, dim):
    return lax.broadcasted_iota(jnp.int32, shape, dim)


def one_hot(mask):
    return jnp.where(mask, 1.0, 0.0).astype(BF16)


def dot(a, b, contract):
    return lax.dot_general(a, b, ((contract[:1], contract[1:]), ((), ())), preferred_element_type=F32)


def kernel(
    x_ref, keep_ref, count_ref, slot_ref, w_hbm, res_ref,
    stream_ref, inverse_ref,
    send_kv, send_q, recv_kv, recv_q, kv0, kv1, kv2, kv3, seen0, seen1, seen2, seen3, q_ref, bias_ref, w_ref,
    m_ref, acc_ref, att_ref, part_ref, pair_ref, half_send, half_p, half_m, near_send, block_p, block_m,
    z_send, z_recv, ssq_ref, ssq_send, ssq_recv,
    a2a_sem, g_send, g_recv, r_send, r_recv, s_sem, w_sem,
):
    kvs, seen = (kv0, kv1, kv2, kv3), (seen0, seen1, seen2, seen3)
    me = lax.axis_index("seq")
    tp = lax.axis_index("tp")
    zz, xx, cc = me >> 3, (me >> 1) & 3, me & 1
    yy, zl = tp >> 1, tp & 1
    y_up, y_down, y_far = (yy + 1) & 3, (yy - 1) & 3, (yy + 2) & 3

    def seq_id(z, x, c):
        return {"seq": (((z & 3) * 4 + (x & 3)) * 2 + c)}

    def tp_id(y, z):
        return {"tp": (y & 3) * 2 + z}

    to_send, to_recv = {}, {}

    def start(copies):
        for key, copy in copies:
            copy.start()
            to_send[key] = to_recv[key] = copy

    def wait_recv(copies):
        for key, copy in copies:
            copy.wait_recv()
            to_recv.pop(key)

    w_copy = pltpu.make_async_copy(w_hbm, w_ref, w_sem)
    w_copy.start()

    barrier = pltpu.get_barrier_semaphore()

    @pl.loop(1, N_SEQ)
    def _(o):
        pl.semaphore_signal(barrier, inc=1, device_id={"seq": (me + o) & 31}, device_id_type=MESH)

    @pl.loop(1, N_TP)
    def _(o):
        pl.semaphore_signal(barrier, inc=1, device_id={"tp": (tp + o) & 7}, device_id_type=MESH)

    f_col, f_row = iota((FRAMES, FRAMES), 0), iota((FRAMES, FRAMES), 1)
    counts, slots = count_ref[...], slot_ref[...]
    starts_col = jnp.sum(jnp.where(f_row < f_col, counts, 0), axis=1, keepdims=True)
    count_col = jnp.sum(jnp.where(f_row == f_col, counts, 0), axis=1, keepdims=True)
    slot_col = jnp.sum(jnp.where(f_row == f_col, slots, 0), axis=1, keepdims=True)

    r_id = iota((N_SEQ * PAIR, 1), 0)
    second = ((r_id >> 3) & 1) == 1

    def own(fl, values):
        return jnp.sum(jnp.where(slot_col == 2 * me + fl, values, 0), axis=0, keepdims=True)

    first_r = jnp.where(second, own(1, starts_col), own(0, starts_col))
    count_r = jnp.where(second, own(1, count_col), own(0, count_col))
    offset_r = (((r_id >> 4) - first_r) & 31) + 32 * (r_id & 7)
    offset_r = jnp.where(offset_r < count_r, offset_r, -1)
    picked = []
    for fl in range(2):
        wanted = jnp.where(second if fl else jnp.logical_not(second), offset_r, -1)
        chosen = one_hot(iota((N_SEQ * PAIR, GRID), 1) == wanted)
        kept = one_hot(iota((GRID, GRID), 0) == keep_ref[fl : fl + 1, :])
        picked.append(dot(chosen, kept, (1, 1)).astype(BF16))
    pick = jnp.concatenate(picked, axis=1)

    def pick_heads(low, high):
        rows = [jnp.concatenate([x_ref[0, h], x_ref[1, h]], axis=0) for h in range(low, high)]
        return dot(pick, jnp.concatenate(rows, axis=1), (1, 0)).astype(BF16).reshape(N_SEQ, PAIR, -1)

    send_kv[...] = pick_heads(HEADS, HEADS + 2)

    pl.semaphore_wait(barrier, N_SEQ - 1 + N_TP - 1)

    def exchange(src, dst, at):
        def send(z, low):
            other = ((zz + z) & 3) * 8 + ((me + low) & 7)
            pltpu.make_async_remote_copy(
                src_ref=src.at[other],
                dst_ref=dst.at[me],
                send_sem=a2a_sem.at[at],
                recv_sem=a2a_sem.at[at + 1],
                device_id={"seq": other},
                device_id_type=MESH,
            ).start()

        @pl.loop(0, 7)
        def _(i):
            send(2, i)
            send(1, i)
            send(3, i)
            send(0, i + 1)

        send(2, 7)
        send(1, 7)
        send(3, 7)

        key, copy = exchange_all(src, dst, at)[0]
        to_send[key] = to_recv[key] = copy

    def exchange_all(src, dst, at):
        copy = pltpu.make_async_remote_copy(
            src_ref=src.at[pl.ds(0, N_SEQ - 1)],
            dst_ref=dst.at[pl.ds(0, N_SEQ - 1)],
            send_sem=a2a_sem.at[at],
            recv_sem=a2a_sem.at[at + 1],
            device_id={"seq": (me + 1) & 31},
            device_id_type=MESH,
        )
        return [((2, 0, at), copy)]

    exchange(send_kv, recv_kv, 0)
    recv_kv[pl.ds(me, 1)] = send_kv[pl.ds(me, 1)]
    send_q[...] = pick_heads(0, HEADS)
    recv_q[pl.ds(me, 1)] = send_q[pl.ds(me, 1)]

    lane = iota((1, N_SEQ * PAIR), 1)
    at_slot = slot_col == (iota((FRAMES, N_SEQ * PAIR), 1) >> 3)
    first_l = jnp.sum(jnp.where(at_slot, starts_col, 0), axis=0, keepdims=True)
    count_l = jnp.sum(jnp.where(at_slot, count_col, 0), axis=0, keepdims=True)
    offset_l = ((me - first_l) & 31) + 32 * (lane & 7)
    row_l = jnp.where(offset_l < count_l, (first_l + offset_l) >> 5, -1)
    place = one_hot(iota((TOK, N_SEQ * PAIR), 0) == row_l)

    wait_recv(exchange_all(send_kv, recv_kv, 0))
    mine = dot(place, recv_kv[...].reshape(N_SEQ * PAIR, 2 * HD), (1, 0)).astype(BF16)
    for c in range(CHUNKS):
        kvs[c][xx, cc, zz] = mine[KEY_AT[c] : KEY_AT[c + 1], :]

    def seq_copy(c, at, src, dst, device):
        return (0, c, at), pltpu.make_async_remote_copy(
            src_ref=src, dst_ref=dst, send_sem=g_send.at[c, at], recv_sem=g_recv.at[c, at],
            device_id=device, device_id_type=MESH,
        )

    def z_one(c):
        ref = kvs[c].at[xx, cc, zz]
        steps = (0, 1, 2) if c in Z_DIRECT else (0, 2)
        return [seq_copy(c, step, ref, ref, seq_id(zz + step + 1, xx, cc)) for step in steps]

    def z_two(c):
        if c in Z_DIRECT:
            return []
        cut = KEY_ROWS[c] // 32 * 16
        up = kvs[c].at[xx, cc, (zz - 1) & 3, pl.ds(0, cut)]
        down = kvs[c].at[xx, cc, (zz + 1) & 3, pl.ds(cut, KEY_ROWS[c] - cut)]
        return [
            seq_copy(c, 1, up, up, seq_id(zz + 1, xx, cc)),
            seq_copy(c, 4, down, down, seq_id(zz - 1, xx, cc)),
        ]

    def gather_z(c):
        wait_recv(z_one(c))
        start(z_two(c))

    def x_one(c):
        ref = kvs[c].at[xx, cc]
        return [seq_copy(c, 2 + step, ref, ref, seq_id(zz, xx + step, cc)) for step in (1, 3)]

    def x_two(c):
        up = kvs[c].at[(xx - 1) & 3, cc, pl.ds(0, 2)]
        down = kvs[c].at[(xx + 1) & 3, cc, pl.ds(2, 2)]
        return [
            seq_copy(c, 6, up, up, seq_id(zz, xx + 1, cc)),
            seq_copy(c, 7, down, down, seq_id(zz, xx - 1, cc)),
        ]

    def sibling(c, step):
        ref = kvs[c].at[(xx + step) & 3, cc]
        return [seq_copy(c, 8 + step, ref, ref, seq_id(zz, xx, 1 - cc))]

    def gather_stage(stage, c):
        if stage == 0:
            start(z_one(c))
        elif stage == 1:
            wait_recv(z_one(c) if c in Z_DIRECT else z_two(c))
            start(x_one(c))
            start(sibling(c, 0))
        elif stage == 2:
            wait_recv(x_one(c))
            start(x_two(c))
            for step in (1, 3):
                start(sibling(c, step))
        elif stage == 3:
            wait_recv(x_two(c))
            start(sibling(c, 2))
        elif stage == 4:
            for step in range(4):
                wait_recv(sibling(c, step))

    def mark_keys():
        lanes = iota((1, HD), 1)
        firsts = jnp.sum(jnp.where(iota((FRAMES, HD), 0) < lanes, count_col, 0), axis=0, keepdims=True)
        firsts = jnp.where(lanes < FRAMES, firsts, FAR)
        q_pos = iota((TOK, 1), 0) * N_SEQ + me
        ends = jnp.min(jnp.where(firsts > q_pos, firsts, FAR), axis=1, keepdims=True)
        bias_ref[...] = jnp.where((firsts == ends) & (firsts < FAR), NEGATIVE, 0.0).astype(BF16)
        for c in range(CHUNKS):
            rows = KEY_ROWS[c]

            @pl.loop(0, N_SEQ)
            def _(i, c=c, rows=rows):
                x, core, z = i >> 3, (i >> 2) & 1, i & 3
                pos = (KEY_AT[c] + iota((rows, 1), 0)) * N_SEQ + (z * 4 + x) * 2 + core
                seen[c][pl.ds(pl.multiple_of(i * rows, 16), rows), :] = one_hot(pos >= firsts)

    def load_queries():
        wait_recv(exchange_all(send_q, recv_q, 2))
        queries = dot(place, recv_q[...].reshape(N_SEQ * PAIR, HEADS * HD), (1, 0)).astype(BF16)
        for a in range(HEADS):
            q_ref[a] = queries[:, a * HD : (a + 1) * HD]

    def attention(j, parts):
        low, high = QUERY_AT[j], QUERY_AT[j + 1]
        rows = HEADS * (high - low)
        q = jnp.concatenate(
            [q_ref[:, low:high, :].reshape(rows, HD), jnp.concatenate([bias_ref[low:high, :]] * HEADS, axis=0)], axis=1
        )
        if 0 in parts:
            m_ref[:rows] = jnp.full((rows, HD), NEGATIVE, F32)
            acc_ref[:rows] = jnp.zeros((rows, 2 * HD), F32)
        for c in parts:
            block = KEY_ROWS[c] * N_SEQ // KEY_BLOCKS[c]
            flat = kvs[c].reshape(KEY_ROWS[c] * N_SEQ, 2 * HD)

            def step(i, c=c, block=block, flat=flat):
                at = pl.multiple_of(i * block, 128)
                keys = jnp.concatenate([flat[pl.ds(at, block), :HD], seen[c][pl.ds(at, block), :]], axis=1)
                values = jnp.concatenate([flat[pl.ds(at, block), HD:], jnp.ones((block, HD), BF16)], axis=1)
                s = dot(q, keys, (1, 1))
                old = m_ref[:rows, :1]
                new = jnp.maximum(old, jnp.max(s, axis=1, keepdims=True))
                p = jnp.exp2((s - new) * SCALE).astype(BF16)
                keep = jnp.exp2((old - new) * SCALE)
                m_ref[:rows] = jnp.broadcast_to(new, (rows, HD))
                acc_ref[:rows] = acc_ref[:rows] * keep + dot(p, values, (1, 0))

            if KEY_BLOCKS[c] == 1:
                step(0)
            else:
                pl.loop(0, KEY_BLOCKS[c])(step)

        if j in parts:
            out = (acc_ref[:rows, :HD] / acc_ref[:rows, HD:]).astype(BF16)
            wide = [out[a * (high - low) : (a + 1) * (high - low)] for a in range(HEADS)]
            att_ref[: high - low] = jnp.concatenate(wide, axis=1)

    def tp_copy(u, at, src, dst, device):
        return (1, u, at), pltpu.make_async_remote_copy(
            src_ref=src, dst_ref=dst, send_sem=r_send.at[u, at], recv_sem=r_recv.at[u, at],
            device_id=device, device_id_type=MESH,
        )

    def far_halves(u):
        if PAIR_FIRST[u]:
            columns = pl.ds(0, WIDTH // 2)
            return [
                tp_copy(u, 0, half_send.at[u, 0], half_p.at[u, :, columns], tp_id(yy + 1, zl)),
                tp_copy(u, 1, half_send.at[u, 1], half_m.at[u, :, columns], tp_id(yy - 1, zl)),
            ]
        return [
            tp_copy(u, 0, part_ref.at[u, 0, y_far], half_p.at[u], tp_id(yy + 1, zl)),
            tp_copy(u, 1, part_ref.at[u, 1, y_far], half_m.at[u], tp_id(yy - 1, zl)),
        ]

    def near_blocks(u):
        if PAIR_FIRST[u]:
            return [
                tp_copy(u, 2, near_send.at[u, 0], block_p.at[u, 0], tp_id(yy + 1, zl)),
                tp_copy(u, 3, near_send.at[u, 1], block_m.at[u, 0], tp_id(yy - 1, zl)),
            ]
        return [
            tp_copy(u, 2, part_ref.at[u, :, y_up], block_p.at[u], tp_id(yy + 1, zl)),
            tp_copy(u, 3, part_ref.at[u, :, y_down], block_m.at[u], tp_id(yy - 1, zl)),
        ]

    def z_pair(u):
        return [tp_copy(u, 4, z_send.at[u], z_recv.at[u], tp_id(yy, 1 - zl))]

    def z_piece(u, step):
        y = (yy + step) & 3
        return [tp_copy(u, 4 + step, part_ref.at[u, 1 - zl, y], pair_ref.at[u, y], tp_id(yy, 1 - zl))]

    def project(j):
        low, high = QUERY_AT[j], QUERY_AT[j + 1]
        for step in (2, 1, 3, 0):
            y = (yy + step) & 3
            w = w_ref[:, pl.ds(pl.multiple_of(y * 2 * WIDTH, 2 * WIDTH), 2 * WIDTH)]
            out = dot(att_ref[: high - low], w, (1, 0)).astype(BF16)
            for n, u in enumerate(UNITS_OF[j]):
                part_ref[u, 0, y] = out[n * UNIT : (n + 1) * UNIT, :WIDTH]
                part_ref[u, 1, y] = out[n * UNIT : (n + 1) * UNIT, WIDTH:]
            for u in UNITS_OF[j]:
                if PAIR_FIRST[u]:
                    start(z_piece(u, step))
                elif step == 2:
                    start(far_halves(u))

    def paired(u, y):
        return part_ref[u, zl, y].astype(F32) + pair_ref[u, y].astype(F32)

    def reduce_pair(u):
        wait_recv(z_piece(u, 2))
        both = paired(u, y_far).astype(BF16)
        half_send[u, 0] = both[:, : WIDTH // 2]
        half_send[u, 1] = both[:, WIDTH // 2 :]
        start(far_halves(u))

    def reduce_near(u):
        if PAIR_FIRST[u]:
            half = WIDTH // 2
            wait_recv(z_piece(u, 1) + z_piece(u, 3) + far_halves(u))
            up, down = paired(u, y_up), paired(u, y_down)
            near_send[u, 0, :, :half] = (up[:, :half] + half_p[u, :, :half].astype(F32)).astype(BF16)
            near_send[u, 0, :, half:] = up[:, half:].astype(BF16)
            near_send[u, 1, :, :half] = down[:, :half].astype(BF16)
            near_send[u, 1, :, half:] = (down[:, half:] + half_m[u, :, :half].astype(F32)).astype(BF16)
        else:
            wait_recv(far_halves(u))
            part_ref[u, 0, y_up] = (part_ref[u, 0, y_up].astype(F32) + half_p[u].astype(F32)).astype(BF16)
            part_ref[u, 1, y_down] = (part_ref[u, 1, y_down].astype(F32) + half_m[u].astype(F32)).astype(BF16)
        start(near_blocks(u))

    def reduce_own(u):
        wait_recv(near_blocks(u))
        rows = pl.ds(u * UNIT, UNIT)

        def total(h):
            return part_ref[u, h, yy].astype(F32) + block_p[u, h].astype(F32) + block_m[u, h].astype(F32)

        if PAIR_FIRST[u]:
            wait_recv(z_piece(u, 0))
            finish(rows, paired(u, yy) + block_p[u, 0].astype(F32) + block_m[u, 0].astype(F32) + res_ref[rows, :].astype(F32))
        else:
            z_send[u] = total(1 - zl).astype(BF16)
            start(z_pair(u))
            stream_ref[rows, :] = total(zl) + res_ref[rows, :].astype(F32)

    def finish(rows, stream):
        stream_ref[rows, :] = stream
        ssq_ref[rows, :] = jnp.broadcast_to(jnp.sum(stream * stream, axis=1, keepdims=True), (UNIT, HD))

    def finish_rows(u):
        if not PAIR_FIRST[u]:
            wait_recv(z_pair(u))
            rows = pl.ds(u * UNIT, UNIT)
            finish(rows, stream_ref[rows, :] + z_recv[u].astype(F32))

    gather_stage(0, 0)
    gather_stage(0, 2)
    gather_stage(0, 1)
    gather_stage(1, 0)
    exchange(send_q, recv_q, 2)
    gather_stage(1, 2)
    mark_keys()
    gather_stage(2, 0)
    gather_stage(1, 1)
    gather_stage(2, 2)
    gather_stage(0, 3)
    gather_stage(3, 0)
    load_queries()
    gather_stage(4, 0)
    attention(0, (0,))
    gather_stage(2, 1)
    w_copy.wait()
    project(0)
    gather_stage(3, 2)
    gather_stage(1, 3)
    gather_stage(3, 1)
    gather_stage(4, 2)
    reduce_near(0)
    gather_stage(4, 1)
    reduce_pair(1)
    attention(1, (0, 1))
    gather_stage(2, 3)
    project(1)
    reduce_near(1)
    reduce_own(0)
    attention(2, (0, 1, 2))
    gather_stage(3, 3)
    project(2)
    gather_stage(4, 3)
    reduce_near(2)
    reduce_pair(3)
    attention(3, (0, 1, 2, 3))
    reduce_near(4)
    reduce_own(1)
    finish_rows(0)
    project(3)
    reduce_pair(5)
    reduce_own(2)
    reduce_near(3)
    reduce_own(4)
    reduce_pair(7)
    reduce_near(6)
    reduce_near(5)
    reduce_own(3)
    reduce_near(7)
    finish_rows(2)
    reduce_own(6)
    finish_rows(4)
    reduce_own(5)
    reduce_own(7)
    finish_rows(6)

    diag = iota((TOK, TOK), 0) == iota((TOK, TOK), 1)
    ssq_row = jnp.sum(jnp.where(diag, ssq_ref[:, :1], 0.0), axis=0, keepdims=True)
    ssq_send[...] = jnp.broadcast_to(ssq_row, (8, TOK))
    ssq_recv[pl.ds(tp, 1)] = ssq_send[...][None]

    for o in (4, 3, 5, 2, 6, 1, 7):
        pltpu.make_async_remote_copy(
            src_ref=ssq_send, dst_ref=ssq_recv.at[tp], send_sem=s_sem.at[0], recv_sem=s_sem.at[1],
            device_id={"tp": (tp + o) & 7}, device_id_type=MESH,
        ).start()

    ssq_all = pltpu.make_async_remote_copy(
        src_ref=ssq_recv.at[pl.ds(0, N_TP - 1)], dst_ref=ssq_recv.at[pl.ds(0, N_TP - 1)],
        send_sem=s_sem.at[0], recv_sem=s_sem.at[1],
        device_id={"tp": (tp + 1) & 7}, device_id_type=MESH,
    )
    for key in to_send:
        to_send[key].wait_send()
    ssq_all.wait_recv()
    sums = jnp.sum(ssq_recv[...], axis=0)[:1, :]
    inverse_row = lax.rsqrt(sums / D + EPSILON)
    inverse = jnp.sum(jnp.where(diag, inverse_row, 0.0), axis=1, keepdims=True)
    inverse_ref[...] = jnp.broadcast_to(inverse, (TOK, HD))
    ssq_all.wait_send()


def normalize(stream_ref, inverse_ref, gain_ref, hid_ref, nrm_ref):
    stream = stream_ref[...]
    gain = gain_ref[...].astype(F32).reshape(1, WIDTH)
    hid_ref[...] = stream.astype(BF16)
    nrm_ref[...] = (stream * inverse_ref[:, :1] * gain).astype(BF16)


def body(frame_grid, keep_rows, kept_count, frame_slot, out_weight, residual, norm_gain):
    vmem = pl.BlockSpec(memory_space=pltpu.VMEM)
    dma = pltpu.SemaphoreType.DMA
    stream, inverse = pl.pallas_call(
        kernel,
        out_shape=[jax.ShapeDtypeStruct((TOK, WIDTH), F32), jax.ShapeDtypeStruct((TOK, HD), F32)],
        in_specs=[vmem] * 4 + [pl.BlockSpec(memory_space=pl.ANY)] + [vmem],
        out_specs=[vmem] * 2,
        scratch_shapes=[
            pltpu.VMEM((N_SEQ, PAIR, 2 * HD), BF16),
            pltpu.VMEM((N_SEQ, PAIR, HEADS * HD), BF16),
            pltpu.VMEM((N_SEQ, PAIR, 2 * HD), BF16),
            pltpu.VMEM((N_SEQ, PAIR, HEADS * HD), BF16),
        ]
        + [pltpu.VMEM((4, 2, 4, rows, 2 * HD), BF16) for rows in KEY_ROWS]
        + [pltpu.VMEM((N_SEQ * rows, HD), BF16) for rows in KEY_ROWS]
        + [
            pltpu.VMEM((HEADS, TOK, HD), BF16),
            pltpu.VMEM((TOK, HD), BF16),
            pltpu.VMEM((HEADS * HD, D), BF16),
            pltpu.VMEM((HEADS * MOST, HD), F32),
            pltpu.VMEM((HEADS * MOST, 2 * HD), F32),
            pltpu.VMEM((MOST, HEADS * HD), BF16),
            pltpu.VMEM((UNITS, 2, 4, UNIT, WIDTH), BF16),
            pltpu.VMEM((UNITS, 4, UNIT, WIDTH), BF16),
            pltpu.VMEM((UNITS, 2, UNIT, WIDTH // 2), BF16),
            pltpu.VMEM((UNITS, UNIT, WIDTH), BF16),
            pltpu.VMEM((UNITS, UNIT, WIDTH), BF16),
            pltpu.VMEM((UNITS, 2, UNIT, WIDTH), BF16),
            pltpu.VMEM((UNITS, 2, UNIT, WIDTH), BF16),
            pltpu.VMEM((UNITS, 2, UNIT, WIDTH), BF16),
            pltpu.VMEM((UNITS, UNIT, WIDTH), BF16),
            pltpu.VMEM((UNITS, UNIT, WIDTH), BF16),
            pltpu.VMEM((TOK, HD), F32),
            pltpu.VMEM((8, TOK), F32),
            pltpu.VMEM((N_TP, 8, TOK), F32),
            dma((4,)),
            dma((CHUNKS, 12)),
            dma((CHUNKS, 12)),
            dma((UNITS, 8)),
            dma((UNITS, 8)),
            dma((2,)),
            dma,
        ],
        compiler_params=pltpu.CompilerParams(
            collective_id=0, has_side_effects=True, vmem_limit_bytes=56 * 1024 * 1024
        ),
        cost_estimate=pl.CostEstimate(flops=5 * 10**9, bytes_accessed=12 * 10**6, transcendentals=5 * 10**6),
    )(
        frame_grid[:, :, 0].transpose(0, 2, 1, 3),
        keep_rows,
        kept_count.reshape(1, FRAMES),
        frame_slot.reshape(1, FRAMES),
        out_weight,
        residual,
    )
    return pl.pallas_call(
        normalize,
        out_shape=[jax.ShapeDtypeStruct((TOK, WIDTH), BF16)] * 2,
        in_specs=[vmem] * 3,
        out_specs=[vmem] * 2,
        cost_estimate=pl.CostEstimate(flops=10**6, bytes_accessed=2 * 10**6, transcendentals=0),
    )(stream, inverse, norm_gain)


def solution(mesh):
    in_specs = (
        P("seq", None, "tp", None, None),
        P("seq", None),
        P(),
        P(),
        P("tp", None),
        P("seq", "tp"),
        P("tp"),
    )
    out_specs = (P("seq", "tp"), P("seq", "tp"))
    return jax.shard_map(body, mesh=mesh, in_specs=in_specs, out_specs=out_specs, check_vma=False)
```

```python
import math

import jax
import jax.numpy as jnp
from jax import lax
from jax.experimental import pallas as pl
from jax.experimental.pallas import tpu as pltpu
from jax.sharding import PartitionSpec as P

D = 8192
HD = 128
HEADS = 4
FRAMES = 64
GRID = 256
TOK = 256
N_SEQ = 32
N_TP = 8
WIDTH = D // N_TP
PAIR = 16
QUERY_AT = (0, 64, 128, 192, 256)
KEY_AT = (0, 80, 144, 208, 256)
CHUNKS = 4
KEY_ROWS = tuple(KEY_AT[i + 1] - KEY_AT[i] for i in range(CHUNKS))
KEY_BLOCKS = (1, 1, 1, 1)
MOST = max(QUERY_AT[i + 1] - QUERY_AT[i] for i in range(CHUNKS))
UNIT = 32
UNITS = TOK // UNIT
PAIR_FIRST = (False, True, False, True, False, True, False, True)
UNITS_OF = ((0, 1), (2, 3), (4, 5), (6, 7))
Z_DIRECT = (0, 1, 2, 3)
NEGATIVE = -1e30
FAR = 1 << 20
EPSILON = 1e-06
SCALE = math.log2(math.e) / math.sqrt(HD)
MESH = pl.DeviceIdType.MESH
F32 = jnp.float32
BF16 = jnp.bfloat16


def iota(shape, dim):
    return lax.broadcasted_iota(jnp.int32, shape, dim)


def one_hot(mask):
    return jnp.where(mask, 1.0, 0.0).astype(BF16)


def dot(a, b, contract):
    return lax.dot_general(a, b, ((contract[:1], contract[1:]), ((), ())), preferred_element_type=F32)


def kernel(
    x_ref, keep_ref, count_ref, slot_ref, w_hbm, res_ref,
    stream_ref, inverse_ref,
    send_kv, send_q, recv_kv, recv_q, kv0, kv1, kv2, kv3, seen0, seen1, seen2, seen3, q_ref, bias_ref, w_ref,
    m_ref, acc_ref, att_ref, part_ref, pair_ref, half_send, half_p, half_m, near_send, block_p, block_m,
    z_send, z_recv, ssq_ref, ssq_send, ssq_recv,
    a2a_sem, g_send, g_recv, r_send, r_recv, s_sem, w_sem,
):
    kvs, seen = (kv0, kv1, kv2, kv3), (seen0, seen1, seen2, seen3)
    me = lax.axis_index("seq")
    tp = lax.axis_index("tp")
    zz, xx, cc = me >> 3, (me >> 1) & 3, me & 1
    yy, zl = tp >> 1, tp & 1
    y_up, y_down, y_far = (yy + 1) & 3, (yy - 1) & 3, (yy + 2) & 3

    def seq_id(z, x, c):
        return {"seq": (((z & 3) * 4 + (x & 3)) * 2 + c)}

    def tp_id(y, z):
        return {"tp": (y & 3) * 2 + z}

    to_send, to_recv = {}, {}

    def start(copies):
        for key, copy in copies:
            copy.start()
            to_send[key] = to_recv[key] = copy

    def wait_recv(copies):
        for key, copy in copies:
            copy.wait_recv()
            to_recv.pop(key)

    w_copy = pltpu.make_async_copy(w_hbm, w_ref, w_sem)
    w_copy.start()

    barrier = pltpu.get_barrier_semaphore()

    def greet(z, low):
        other = ((zz + z) & 3) * 8 + ((me + low) & 7)
        pl.semaphore_signal(barrier, inc=1, device_id={"seq": other}, device_id_type=MESH)

    for z in (2, 1, 3):
        pl.loop(0, 8)(lambda i, z=z: greet(z, (i + 4) & 7))
    pl.loop(1, 8)(lambda i: greet(0, i))

    @pl.loop(1, N_TP)
    def _(o):
        pl.semaphore_signal(barrier, inc=1, device_id={"tp": (tp + o) & 7}, device_id_type=MESH)

    f_col, f_row = iota((FRAMES, FRAMES), 0), iota((FRAMES, FRAMES), 1)
    counts, slots = count_ref[...], slot_ref[...]
    starts_col = jnp.sum(jnp.where(f_row < f_col, counts, 0), axis=1, keepdims=True)
    count_col = jnp.sum(jnp.where(f_row == f_col, counts, 0), axis=1, keepdims=True)
    slot_col = jnp.sum(jnp.where(f_row == f_col, slots, 0), axis=1, keepdims=True)

    r_id = iota((N_SEQ * PAIR, 1), 0)
    second = ((r_id >> 3) & 1) == 1

    def own(fl, values):
        return jnp.sum(jnp.where(slot_col == 2 * me + fl, values, 0), axis=0, keepdims=True)

    first_r = jnp.where(second, own(1, starts_col), own(0, starts_col))
    count_r = jnp.where(second, own(1, count_col), own(0, count_col))
    offset_r = (((r_id >> 4) - first_r) & 31) + 32 * (r_id & 7)
    offset_r = jnp.where(offset_r < count_r, offset_r, -1)
    picked = []
    for fl in range(2):
        wanted = jnp.where(second if fl else jnp.logical_not(second), offset_r, -1)
        chosen = one_hot(iota((N_SEQ * PAIR, GRID), 1) == wanted)
        kept = one_hot(iota((GRID, GRID), 0) == keep_ref[fl : fl + 1, :])
        picked.append(dot(chosen, kept, (1, 1)).astype(BF16))
    pick = jnp.concatenate(picked, axis=1)

    def pick_heads(low, high):
        rows = [jnp.concatenate([x_ref[0, h], x_ref[1, h]], axis=0) for h in range(low, high)]
        return dot(pick, jnp.concatenate(rows, axis=1), (1, 0)).astype(BF16).reshape(N_SEQ, PAIR, -1)

    send_kv[...] = pick_heads(HEADS, HEADS + 2)

    pl.semaphore_wait(barrier, N_SEQ - 1 + N_TP - 1)

    def exchange(src, dst, at):
        def send(z, low):
            other = ((zz + z) & 3) * 8 + ((me + low) & 7)
            pltpu.make_async_remote_copy(
                src_ref=src.at[other],
                dst_ref=dst.at[me],
                send_sem=a2a_sem.at[at],
                recv_sem=a2a_sem.at[at + 1],
                device_id={"seq": other},
                device_id_type=MESH,
            ).start()

        @pl.loop(0, 7)
        def _(i):
            send(2, i)
            send(1, i)
            send(3, i)
            send(0, i + 1)

        send(2, 7)
        send(1, 7)
        send(3, 7)

        key, copy = exchange_all(src, dst, at)[0]
        to_send[key] = to_recv[key] = copy

    def exchange_all(src, dst, at):
        copy = pltpu.make_async_remote_copy(
            src_ref=src.at[pl.ds(0, N_SEQ - 1)],
            dst_ref=dst.at[pl.ds(0, N_SEQ - 1)],
            send_sem=a2a_sem.at[at],
            recv_sem=a2a_sem.at[at + 1],
            device_id={"seq": (me + 1) & 31},
            device_id_type=MESH,
        )
        return [((2, 0, at), copy)]

    exchange(send_kv, recv_kv, 0)
    recv_kv[pl.ds(me, 1)] = send_kv[pl.ds(me, 1)]
    send_q[...] = pick_heads(0, HEADS)
    recv_q[pl.ds(me, 1)] = send_q[pl.ds(me, 1)]

    lane = iota((1, N_SEQ * PAIR), 1)
    at_slot = slot_col == (iota((FRAMES, N_SEQ * PAIR), 1) >> 3)
    first_l = jnp.sum(jnp.where(at_slot, starts_col, 0), axis=0, keepdims=True)
    count_l = jnp.sum(jnp.where(at_slot, count_col, 0), axis=0, keepdims=True)
    offset_l = ((me - first_l) & 31) + 32 * (lane & 7)
    row_l = jnp.where(offset_l < count_l, (first_l + offset_l) >> 5, -1)
    place = one_hot(iota((TOK, N_SEQ * PAIR), 0) == row_l)

    wait_recv(exchange_all(send_kv, recv_kv, 0))
    mine = dot(place, recv_kv[...].reshape(N_SEQ * PAIR, 2 * HD), (1, 0)).astype(BF16)
    for c in range(CHUNKS):
        kvs[c][xx, cc, zz] = mine[KEY_AT[c] : KEY_AT[c + 1], :]

    def seq_copy(c, at, src, dst, device):
        return (0, c, at), pltpu.make_async_remote_copy(
            src_ref=src, dst_ref=dst, send_sem=g_send.at[c, at], recv_sem=g_recv.at[c, at],
            device_id=device, device_id_type=MESH,
        )

    def z_one(c):
        ref = kvs[c].at[xx, cc, zz]
        steps = (0, 1, 2) if c in Z_DIRECT else (0, 2)
        return [seq_copy(c, step, ref, ref, seq_id(zz + step + 1, xx, cc)) for step in steps]

    def z_two(c):
        if c in Z_DIRECT:
            return []
        cut = KEY_ROWS[c] // 32 * 16
        up = kvs[c].at[xx, cc, (zz - 1) & 3, pl.ds(0, cut)]
        down = kvs[c].at[xx, cc, (zz + 1) & 3, pl.ds(cut, KEY_ROWS[c] - cut)]
        return [
            seq_copy(c, 1, up, up, seq_id(zz + 1, xx, cc)),
            seq_copy(c, 4, down, down, seq_id(zz - 1, xx, cc)),
        ]

    def gather_z(c):
        wait_recv(z_one(c))
        start(z_two(c))

    def x_one(c):
        ref = kvs[c].at[xx, cc]
        return [seq_copy(c, 2 + step, ref, ref, seq_id(zz, xx + step, cc)) for step in (1, 3)]

    def x_two(c):
        up = kvs[c].at[(xx - 1) & 3, cc, pl.ds(0, 2)]
        down = kvs[c].at[(xx + 1) & 3, cc, pl.ds(2, 2)]
        return [
            seq_copy(c, 6, up, up, seq_id(zz, xx + 1, cc)),
            seq_copy(c, 7, down, down, seq_id(zz, xx - 1, cc)),
        ]

    def sibling(c, step):
        ref = kvs[c].at[(xx + step) & 3, cc]
        return [seq_copy(c, 8 + step, ref, ref, seq_id(zz, xx, 1 - cc))]

    def gather_stage(stage, c):
        if stage == 0:
            start(z_one(c))
        elif stage == 1:
            wait_recv(z_one(c) if c in Z_DIRECT else z_two(c))
            start(x_one(c))
            start(sibling(c, 0))
        elif stage == 2:
            wait_recv(x_one(c))
            start(x_two(c))
            for step in (1, 3):
                start(sibling(c, step))
        elif stage == 3:
            wait_recv(x_two(c))
            start(sibling(c, 2))
        elif stage == 4:
            for step in range(4):
                wait_recv(sibling(c, step))

    def mark_keys():
        lanes = iota((1, HD), 1)
        firsts = jnp.sum(jnp.where(iota((FRAMES, HD), 0) < lanes, count_col, 0), axis=0, keepdims=True)
        firsts = jnp.where(lanes < FRAMES, firsts, FAR)
        q_pos = iota((TOK, 1), 0) * N_SEQ + me
        ends = jnp.min(jnp.where(firsts > q_pos, firsts, FAR), axis=1, keepdims=True)
        bias_ref[...] = jnp.where((firsts == ends) & (firsts < FAR), NEGATIVE, 0.0).astype(BF16)
        for c in range(CHUNKS):
            rows = KEY_ROWS[c]

            @pl.loop(0, N_SEQ)
            def _(i, c=c, rows=rows):
                x, core, z = i >> 3, (i >> 2) & 1, i & 3
                pos = (KEY_AT[c] + iota((rows, 1), 0)) * N_SEQ + (z * 4 + x) * 2 + core
                seen[c][pl.ds(pl.multiple_of(i * rows, 16), rows), :] = one_hot(pos >= firsts)

    def load_queries():
        wait_recv(exchange_all(send_q, recv_q, 2))
        queries = dot(place, recv_q[...].reshape(N_SEQ * PAIR, HEADS * HD), (1, 0)).astype(BF16)
        for a in range(HEADS):
            q_ref[a] = queries[:, a * HD : (a + 1) * HD]

    def attention(j, parts):
        low, high = QUERY_AT[j], QUERY_AT[j + 1]
        rows = HEADS * (high - low)
        q = jnp.concatenate(
            [q_ref[:, low:high, :].reshape(rows, HD), jnp.concatenate([bias_ref[low:high, :]] * HEADS, axis=0)], axis=1
        )
        if 0 in parts:
            m_ref[:rows] = jnp.full((rows, HD), NEGATIVE, F32)
            acc_ref[:rows] = jnp.zeros((rows, 2 * HD), F32)
        for c in parts:
            block = KEY_ROWS[c] * N_SEQ // KEY_BLOCKS[c]
            flat = kvs[c].reshape(KEY_ROWS[c] * N_SEQ, 2 * HD)

            def step(i, c=c, block=block, flat=flat):
                at = pl.multiple_of(i * block, 128)
                keys = jnp.concatenate([flat[pl.ds(at, block), :HD], seen[c][pl.ds(at, block), :]], axis=1)
                values = jnp.concatenate([flat[pl.ds(at, block), HD:], jnp.ones((block, HD), BF16)], axis=1)
                s = dot(q, keys, (1, 1))
                old = m_ref[:rows, :1]
                new = jnp.maximum(old, jnp.max(s, axis=1, keepdims=True))
                p = jnp.exp2((s - new) * SCALE).astype(BF16)
                keep = jnp.exp2((old - new) * SCALE)
                m_ref[:rows] = jnp.broadcast_to(new, (rows, HD))
                acc_ref[:rows] = acc_ref[:rows] * keep + dot(p, values, (1, 0))

            if KEY_BLOCKS[c] == 1:
                step(0)
            else:
                pl.loop(0, KEY_BLOCKS[c])(step)

        if j in parts:
            out = (acc_ref[:rows, :HD] / acc_ref[:rows, HD:]).astype(BF16)
            wide = [out[a * (high - low) : (a + 1) * (high - low)] for a in range(HEADS)]
            att_ref[: high - low] = jnp.concatenate(wide, axis=1)

    def tp_copy(u, at, src, dst, device):
        return (1, u, at), pltpu.make_async_remote_copy(
            src_ref=src, dst_ref=dst, send_sem=r_send.at[u, at], recv_sem=r_recv.at[u, at],
            device_id=device, device_id_type=MESH,
        )

    def far_halves(u):
        if PAIR_FIRST[u]:
            columns = pl.ds(0, WIDTH // 2)
            return [
                tp_copy(u, 0, half_send.at[u, 0], half_p.at[u, :, columns], tp_id(yy + 1, zl)),
                tp_copy(u, 1, half_send.at[u, 1], half_m.at[u, :, columns], tp_id(yy - 1, zl)),
            ]
        return [
            tp_copy(u, 0, part_ref.at[u, 0, y_far], half_p.at[u], tp_id(yy + 1, zl)),
            tp_copy(u, 1, part_ref.at[u, 1, y_far], half_m.at[u], tp_id(yy - 1, zl)),
        ]

    def near_blocks(u):
        if PAIR_FIRST[u]:
            return [
                tp_copy(u, 2, near_send.at[u, 0], block_p.at[u, 0], tp_id(yy + 1, zl)),
                tp_copy(u, 3, near_send.at[u, 1], block_m.at[u, 0], tp_id(yy - 1, zl)),
            ]
        return [
            tp_copy(u, 2, part_ref.at[u, :, y_up], block_p.at[u], tp_id(yy + 1, zl)),
            tp_copy(u, 3, part_ref.at[u, :, y_down], block_m.at[u], tp_id(yy - 1, zl)),
        ]

    def z_pair(u):
        return [tp_copy(u, 4, z_send.at[u], z_recv.at[u], tp_id(yy, 1 - zl))]

    def z_piece(u, step):
        y = (yy + step) & 3
        return [tp_copy(u, 4 + step, part_ref.at[u, 1 - zl, y], pair_ref.at[u, y], tp_id(yy, 1 - zl))]

    def project(j):
        low, high = QUERY_AT[j], QUERY_AT[j + 1]
        for step in (2, 1, 3, 0):
            y = (yy + step) & 3
            w = w_ref[:, pl.ds(pl.multiple_of(y * 2 * WIDTH, 2 * WIDTH), 2 * WIDTH)]
            out = dot(att_ref[: high - low], w, (1, 0)).astype(BF16)
            for n, u in enumerate(UNITS_OF[j]):
                part_ref[u, 0, y] = out[n * UNIT : (n + 1) * UNIT, :WIDTH]
                part_ref[u, 1, y] = out[n * UNIT : (n + 1) * UNIT, WIDTH:]
            for u in UNITS_OF[j]:
                if PAIR_FIRST[u]:
                    start(z_piece(u, step))
                elif step == 2:
                    start(far_halves(u))

    def paired(u, y):
        return part_ref[u, zl, y].astype(F32) + pair_ref[u, y].astype(F32)

    def reduce_pair(u):
        wait_recv(z_piece(u, 2))
        both = paired(u, y_far).astype(BF16)
        half_send[u, 0] = both[:, : WIDTH // 2]
        half_send[u, 1] = both[:, WIDTH // 2 :]
        start(far_halves(u))

    def reduce_near(u):
        if PAIR_FIRST[u]:
            half = WIDTH // 2
            wait_recv(z_piece(u, 1) + z_piece(u, 3) + far_halves(u))
            up, down = paired(u, y_up), paired(u, y_down)
            near_send[u, 0, :, :half] = (up[:, :half] + half_p[u, :, :half].astype(F32)).astype(BF16)
            near_send[u, 0, :, half:] = up[:, half:].astype(BF16)
            near_send[u, 1, :, :half] = down[:, :half].astype(BF16)
            near_send[u, 1, :, half:] = (down[:, half:] + half_m[u, :, :half].astype(F32)).astype(BF16)
        else:
            wait_recv(far_halves(u))
            part_ref[u, 0, y_up] = (part_ref[u, 0, y_up].astype(F32) + half_p[u].astype(F32)).astype(BF16)
            part_ref[u, 1, y_down] = (part_ref[u, 1, y_down].astype(F32) + half_m[u].astype(F32)).astype(BF16)
        start(near_blocks(u))

    def reduce_own(u):
        wait_recv(near_blocks(u))
        rows = pl.ds(u * UNIT, UNIT)

        def total(h):
            return part_ref[u, h, yy].astype(F32) + block_p[u, h].astype(F32) + block_m[u, h].astype(F32)

        if PAIR_FIRST[u]:
            wait_recv(z_piece(u, 0))
            finish(rows, paired(u, yy) + block_p[u, 0].astype(F32) + block_m[u, 0].astype(F32) + res_ref[rows, :].astype(F32))
        else:
            z_send[u] = total(1 - zl).astype(BF16)
            start(z_pair(u))
            stream_ref[rows, :] = total(zl) + res_ref[rows, :].astype(F32)

    def finish(rows, stream):
        stream_ref[rows, :] = stream
        ssq_ref[rows, :] = jnp.broadcast_to(jnp.sum(stream * stream, axis=1, keepdims=True), (UNIT, HD))

    def finish_rows(u):
        if not PAIR_FIRST[u]:
            wait_recv(z_pair(u))
            rows = pl.ds(u * UNIT, UNIT)
            finish(rows, stream_ref[rows, :] + z_recv[u].astype(F32))

    gather_stage(0, 0)
    gather_stage(0, 2)
    gather_stage(0, 1)
    gather_stage(1, 0)
    exchange(send_q, recv_q, 2)
    gather_stage(1, 2)
    mark_keys()
    gather_stage(2, 0)
    gather_stage(1, 1)
    gather_stage(2, 2)
    gather_stage(0, 3)
    gather_stage(3, 0)
    load_queries()
    gather_stage(4, 0)
    attention(0, (0,))
    gather_stage(2, 1)
    w_copy.wait()
    project(0)
    gather_stage(3, 2)
    gather_stage(1, 3)
    gather_stage(3, 1)
    gather_stage(4, 2)
    reduce_near(0)
    gather_stage(4, 1)
    reduce_pair(1)
    attention(1, (0, 1))
    gather_stage(2, 3)
    project(1)
    reduce_near(1)
    reduce_own(0)
    attention(2, (0, 1, 2))
    gather_stage(3, 3)
    project(2)
    gather_stage(4, 3)
    reduce_near(2)
    reduce_pair(3)
    attention(3, (0, 1, 2, 3))
    reduce_near(4)
    reduce_own(1)
    finish_rows(0)
    project(3)
    reduce_pair(5)
    reduce_own(2)
    reduce_near(3)
    reduce_own(4)
    reduce_pair(7)
    reduce_near(6)
    reduce_near(5)
    reduce_own(3)
    reduce_near(7)
    finish_rows(2)
    reduce_own(6)
    finish_rows(4)
    reduce_own(5)
    reduce_own(7)
    finish_rows(6)

    diag = iota((TOK, TOK), 0) == iota((TOK, TOK), 1)
    ssq_row = jnp.sum(jnp.where(diag, ssq_ref[:, :1], 0.0), axis=0, keepdims=True)
    ssq_send[...] = jnp.broadcast_to(ssq_row, (8, TOK))
    ssq_recv[pl.ds(tp, 1)] = ssq_send[...][None]

    for o in (4, 3, 5, 2, 6, 1, 7):
        pltpu.make_async_remote_copy(
            src_ref=ssq_send, dst_ref=ssq_recv.at[tp], send_sem=s_sem.at[0], recv_sem=s_sem.at[1],
            device_id={"tp": (tp + o) & 7}, device_id_type=MESH,
        ).start()

    ssq_all = pltpu.make_async_remote_copy(
        src_ref=ssq_recv.at[pl.ds(0, N_TP - 1)], dst_ref=ssq_recv.at[pl.ds(0, N_TP - 1)],
        send_sem=s_sem.at[0], recv_sem=s_sem.at[1],
        device_id={"tp": (tp + 1) & 7}, device_id_type=MESH,
    )
    for key in to_send:
        to_send[key].wait_send()
    ssq_all.wait_recv()
    sums = jnp.sum(ssq_recv[...], axis=0)[:1, :]
    inverse_row = lax.rsqrt(sums / D + EPSILON)
    inverse = jnp.sum(jnp.where(diag, inverse_row, 0.0), axis=1, keepdims=True)
    inverse_ref[...] = jnp.broadcast_to(inverse, (TOK, HD))
    ssq_all.wait_send()


def normalize(stream_ref, inverse_ref, gain_ref, hid_ref, nrm_ref):
    stream = stream_ref[...]
    gain = gain_ref[...].astype(F32).reshape(1, WIDTH)
    hid_ref[...] = stream.astype(BF16)
    nrm_ref[...] = (stream * inverse_ref[:, :1] * gain).astype(BF16)


def body(frame_grid, keep_rows, kept_count, frame_slot, out_weight, residual, norm_gain):
    vmem = pl.BlockSpec(memory_space=pltpu.VMEM)
    dma = pltpu.SemaphoreType.DMA
    stream, inverse = pl.pallas_call(
        kernel,
        out_shape=[jax.ShapeDtypeStruct((TOK, WIDTH), F32), jax.ShapeDtypeStruct((TOK, HD), F32)],
        in_specs=[vmem] * 4 + [pl.BlockSpec(memory_space=pl.ANY)] + [vmem],
        out_specs=[vmem] * 2,
        scratch_shapes=[
            pltpu.VMEM((N_SEQ, PAIR, 2 * HD), BF16),
            pltpu.VMEM((N_SEQ, PAIR, HEADS * HD), BF16),
            pltpu.VMEM((N_SEQ, PAIR, 2 * HD), BF16),
            pltpu.VMEM((N_SEQ, PAIR, HEADS * HD), BF16),
        ]
        + [pltpu.VMEM((4, 2, 4, rows, 2 * HD), BF16) for rows in KEY_ROWS]
        + [pltpu.VMEM((N_SEQ * rows, HD), BF16) for rows in KEY_ROWS]
        + [
            pltpu.VMEM((HEADS, TOK, HD), BF16),
            pltpu.VMEM((TOK, HD), BF16),
            pltpu.VMEM((HEADS * HD, D), BF16),
            pltpu.VMEM((HEADS * MOST, HD), F32),
            pltpu.VMEM((HEADS * MOST, 2 * HD), F32),
            pltpu.VMEM((MOST, HEADS * HD), BF16),
            pltpu.VMEM((UNITS, 2, 4, UNIT, WIDTH), BF16),
            pltpu.VMEM((UNITS, 4, UNIT, WIDTH), BF16),
            pltpu.VMEM((UNITS, 2, UNIT, WIDTH // 2), BF16),
            pltpu.VMEM((UNITS, UNIT, WIDTH), BF16),
            pltpu.VMEM((UNITS, UNIT, WIDTH), BF16),
            pltpu.VMEM((UNITS, 2, UNIT, WIDTH), BF16),
            pltpu.VMEM((UNITS, 2, UNIT, WIDTH), BF16),
            pltpu.VMEM((UNITS, 2, UNIT, WIDTH), BF16),
            pltpu.VMEM((UNITS, UNIT, WIDTH), BF16),
            pltpu.VMEM((UNITS, UNIT, WIDTH), BF16),
            pltpu.VMEM((TOK, HD), F32),
            pltpu.VMEM((8, TOK), F32),
            pltpu.VMEM((N_TP, 8, TOK), F32),
            dma((4,)),
            dma((CHUNKS, 12)),
            dma((CHUNKS, 12)),
            dma((UNITS, 8)),
            dma((UNITS, 8)),
            dma((2,)),
            dma,
        ],
        compiler_params=pltpu.CompilerParams(
            collective_id=0, has_side_effects=True, vmem_limit_bytes=56 * 1024 * 1024
        ),
        cost_estimate=pl.CostEstimate(flops=5 * 10**9, bytes_accessed=12 * 10**6, transcendentals=5 * 10**6),
    )(
        frame_grid[:, :, 0].transpose(0, 2, 1, 3),
        keep_rows,
        kept_count.reshape(1, FRAMES),
        frame_slot.reshape(1, FRAMES),
        out_weight,
        residual,
    )
    return pl.pallas_call(
        normalize,
        out_shape=[jax.ShapeDtypeStruct((TOK, WIDTH), BF16)] * 2,
        in_specs=[vmem] * 3,
        out_specs=[vmem] * 2,
        cost_estimate=pl.CostEstimate(flops=10**6, bytes_accessed=2 * 10**6, transcendentals=0),
    )(stream, inverse, norm_gain)


def solution(mesh):
    in_specs = (
        P("seq", None, "tp", None, None),
        P("seq", None),
        P(),
        P(),
        P("tp", None),
        P("seq", "tp"),
        P("tp"),
    )
    out_specs = (P("seq", "tp"), P("seq", "tp"))
    return jax.shard_map(body, mesh=mesh, in_specs=in_specs, out_specs=out_specs, check_vma=False)
```
